256 devices in a mesh: seq: 64 (over y_lo, x, z), dp: 4 (over y_hi, core).
Axes of the slice: x: 4, y: 4 (y_hi: 2, y_lo: 2; y = y_hi * 2 + y_lo), z: 8, core: 2. Of those that a mesh axis runs over, the one named last changes fastest.
Arguments:
- signal: float32 [4, 65536, 384], P('dp', 'seq'), may hold values from -6 to 6
- gate_values: float32 [4, 65536, 384], P('dp', 'seq'), may hold values from -6 to 6
- cotangent: float32 [4, 65536, 384], P('dp', 'seq'), may hold values from -6 to 6
- kernel: float32 [128, 512, 384], P(None, 'seq'), may hold values from -6 to 6
- first_factor: float32 [128, 128], replicated, may hold values from -0.5 to 0.5
- second_factor: float32 [512, 512], replicated, may hold values from -0.25 to 0.25
Outputs:
- grad_signal: float32 [4, 65536, 384], P('dp', 'seq')
- grad_gates: float32 [4, 65536, 384], P('dp', 'seq')
- grad_kernel: float32 [128, 512, 384], P('dp', 'seq')
- grad_first: float32 [128, 128], replicated
- grad_second: float32 [512, 512], replicated
The draws below stay inside these ranges and needn't reach their ends.
All inputs are finite; a program needn't handle non-finite values.
Results may differ from the reference program's by a relative error of at most 0.000071.
Values sent between devices are 32-bit elements; how exact they have to be, the bound alone decides.
No kernel may reach another device: no remote copies, remote signals or barrier semaphores. Data moves between devices by JAX's collectives and lax.ppermute only.
A program may use at most 128 MiB of HBM per device.

```python
import math
import jax
import jax.numpy as jnp
from jax import lax

BLOCKS = 128
BLOCK = 512
CHANNELS = 384
LENGTH = 65536
SEQS = 4


def level_of(rng, shape, split, least, top_value):
    loudness, own = 1.0, jax.random.fold_in(rng, 6)
    for position, parts in split:
        draws = jnp.exp(jax.random.uniform(jax.random.fold_in(own, position), (parts,), jnp.float32, least / len(split), top_value / len(split)))
        loudness = loudness * jnp.repeat(draws, shape[position] // parts).reshape([-1 if axis == position else 1 for axis in range(len(shape))])
    return loudness


def gaussian(own_key, extent, width, bound, cuts=(), kind=jnp.bfloat16):
    values = width * jax.random.normal(own_key, extent, jnp.float32)
    if cuts:
        values = values * level_of(own_key, extent, cuts, -0.22, 0.18)
    return jnp.clip(values, -bound, bound).astype(kind)


def setup_inputs(seed: int = 0) -> dict:
    splits = jax.random.split(jax.random.key(seed), 7)
    signal = gaussian(splits[0], (SEQS, LENGTH, CHANNELS), 1.0, 6.0, ((0, 4), (1, 64)), jnp.float32)
    gate_values = gaussian(splits[1], (SEQS, LENGTH, CHANNELS), 1.0, 6.0, ((0, 4), (1, 64)), jnp.float32)
    cotangent = gaussian(splits[2], (SEQS, LENGTH, CHANNELS), 1.0, 6.0, ((0, 4), (1, 64)), jnp.float32)
    kernel = gaussian(splits[3], (BLOCKS, BLOCK, CHANNELS), 1.0, 6.0, ((1, 64),), jnp.float32)
    first_factor = gaussian(splits[4], (BLOCKS, BLOCKS), BLOCKS ** -0.5, 0.5, (), jnp.float32)
    second_factor = gaussian(splits[5], (BLOCK, BLOCK), BLOCK ** -0.5, 0.25, (), jnp.float32)
    return dict(signal=signal, gate_values=gate_values, cotangent=cotangent, kernel=kernel, first_factor=first_factor, second_factor=second_factor)


def forward(signal, kernel, first_factor, second_factor):
    highest = lax.Precision.HIGHEST
    source = signal.reshape(SEQS, BLOCKS, BLOCK, CHANNELS)
    section = jnp.einsum('bijc,kj->bikc', source, second_factor, precision=highest)
    spectrum = jnp.einsum('mi,bikc->bmkc', first_factor, section, precision=highest)
    weighted = kernel[None] * spectrum
    back = jnp.einsum('mi,bmkc->bikc', first_factor, weighted, precision=highest)
    mixed = jnp.einsum('bikc,kj->bijc', back, second_factor, precision=highest)
    return mixed.reshape(SEQS, LENGTH, CHANNELS)

def reference(signal, gate_values, cotangent, kernel, first_factor, second_factor):

    def layer(source, gating, weights, first, second):
        return gating * forward(source, weights, first, second)
    output, pullback = jax.vjp(layer, signal, gate_values, kernel, first_factor, second_factor)
    grad_signal, grad_gates, grad_kernel, grad_first, grad_second = pullback(cotangent)
    first_scale = 1.0 / math.sqrt(SEQS * BLOCK * CHANNELS)
    second_scale = 1.0 / math.sqrt(SEQS * BLOCKS * CHANNELS)
    return (grad_signal, grad_gates, grad_kernel, grad_first * first_scale, grad_second * second_scale)
```

```python
import math

import jax
import jax.numpy as jnp
from jax import lax
from jax.experimental import pallas as pl
from jax.experimental.pallas import tpu as pltpu
from jax.sharding import Mesh, PartitionSpec as P

F32 = jnp.float32
BF16 = jnp.bfloat16
VMEM = pl.BlockSpec(memory_space=pltpu.VMEM)
PARAMS = pltpu.CompilerParams(vmem_limit_bytes=48 * 1024 * 1024)


def halves(value):
    high = value.astype(BF16)
    return high, (value - high.astype(F32)).astype(BF16)


def product(left, right, dims):
    one = lambda a, b: lax.dot_general(a, b, (dims, ((), ())), preferred_element_type=F32)
    return one(left[0], right[0]) + (one(left[0], right[1]) + one(left[1], right[0]))


NN = ((1,), (0,))
TN = ((0,), (0,))
NT = ((1,), (1,))


def enter_kernel(x_ref, s_ref, out_ref):
    rows, block, channels = x_ref.shape
    second = halves(s_ref[...])
    for row in range(rows):
        got = product(second, halves(x_ref[row]), NN)
        out_ref[:, row] = got.reshape(out_ref.shape[0], out_ref.shape[2], channels)


def enter_gated_kernel(g_ref, c_ref, s_ref, out_ref):
    rows, block, channels = g_ref.shape
    second = halves(s_ref[...])
    for row in range(rows):
        got = product(second, halves(g_ref[row] * c_ref[row]), NN)
        out_ref[:, row] = got.reshape(out_ref.shape[0], out_ref.shape[2], channels)


def forward_kernel(a_ref, k_ref, f_ref, z_ref, v_ref):
    first = halves(f_ref[...])
    for k in range(a_ref.shape[1]):
        z = product(first, halves(a_ref[:, k]), NN)
        z_ref[:, k] = z
        v_ref[:, k] = product(first, halves(k_ref[:, k] * z), TN)


def backward_kernel(a_ref, d_ref, k_ref, z_ref, f_ref, da_ref, gk_ref, gf_ref):
    first = halves(f_ref[...])
    total = jnp.zeros(gf_ref.shape, F32)
    for k in range(a_ref.shape[1]):
        dv = halves(d_ref[:, k])
        dw = product(first, dv, NN)
        z = z_ref[:, k]
        weight = k_ref[:, k]
        gk_ref[:, k] = dw * z
        dz = halves(weight * dw)
        da_ref[:, k] = product(first, dz, TN)
        total += product(halves(weight * z), dv, NT) + product(dz, halves(a_ref[:, k]), NT)
    gf_ref[...] = total


def leave_gates_kernel(v_ref, g_ref, c_ref, s_ref, gg_ref, gs_ref):
    rows, block, channels = g_ref.shape
    second = halves(s_ref[...])
    total = jnp.zeros(gs_ref.shape, F32)
    for row in range(rows):
        v = halves(v_ref[:, row].reshape(block, channels))
        gg_ref[row] = c_ref[row] * product(second, v, TN)
        total += product(v, halves(g_ref[row] * c_ref[row]), NT)
    gs_ref[...] = total


def leave_signal_kernel(d_ref, x_ref, s_ref, gx_ref, gs_ref):
    rows, block, channels = x_ref.shape
    second = halves(s_ref[...])
    total = jnp.zeros(gs_ref.shape, F32)
    for row in range(rows):
        d = halves(d_ref[:, row].reshape(block, channels))
        gx_ref[row] = product(second, d, TN)
        total += product(d, halves(x_ref[row]), NT)
    gs_ref[...] = total


def call(kernel, outs, *args):
    return pl.pallas_call(
        kernel,
        out_shape=[jax.ShapeDtypeStruct(shape, F32) for shape in outs],
        in_specs=[VMEM] * len(args),
        out_specs=[VMEM] * len(outs),
        compiler_params=PARAMS,
    )(*args)


def exchange(data, axes):
    return lax.all_to_all(data, axes, split_axis=0, concat_axis=0, tiled=True)


def scatter_sum(data, axes):
    parts = lax.axis_size(axes)
    got = exchange(data, axes)
    return jnp.sum(got.reshape((parts, got.shape[0] // parts) + got.shape[1:]), axis=0)


def gather(data, axes):
    parts = lax.axis_size(axes)
    return exchange(jnp.broadcast_to(data[None], (parts,) + data.shape).reshape((parts * data.shape[0],) + data.shape[1:]), axes)


def total_of(data, stages):
    for axes in stages:
        data = scatter_sum(data, axes)
    for axes in reversed(stages):
        data = gather(data, axes)
    return data


def solution(mesh):
    seq = ("near", "x", "z")
    dp = ("far", "core")
    shape = dict(mesh.shape)
    near = 2
    xs = 4
    fine = Mesh(
        mesh.devices.reshape(near, xs, shape["seq"] // (near * xs), shape["dp"] // 2, 2),
        seq + dp,
    )

    def body(signal, gate_values, cotangent, kernel, first_factor, second_factor):
        blocks = first_factor.shape[0]
        block = second_factor.shape[0]
        channels = signal.shape[2]
        peers = lax.axis_size(seq)
        rows = signal.shape[1] // block
        width = block // peers
        send = (peers, rows, width, channels)
        side = (blocks, width, channels)
        place = (rows, block, channels)
        source = signal.reshape(place)
        gating = gate_values.reshape(place)
        upstream = cotangent.reshape(place)
        (section,) = call(enter_kernel, [send], source, second_factor)
        section = exchange(section, seq).reshape(side)
        (grad_back,) = call(enter_gated_kernel, [send], gating, upstream, second_factor)
        grad_back = exchange(grad_back, seq).reshape(side)
        spectrum, back = call(forward_kernel, [side, side], section, kernel, first_factor)
        back = exchange(back.reshape(send), seq)
        grad_section, grad_kernel, grad_first = call(
            backward_kernel, [side, side, (blocks, blocks)], section, grad_back, kernel, spectrum, first_factor
        )
        grad_section = exchange(grad_section.reshape(send), seq)
        grad_kernel = scatter_sum(grad_kernel, dp)
        grad_gate, second_one = call(
            leave_gates_kernel, [place, (block, block)], back, gating, upstream, second_factor
        )
        grad_source, second_two = call(
            leave_signal_kernel, [place, (block, block)], grad_section, source, second_factor
        )
        sequences = lax.axis_size(dp)
        first_scale = 1.0 / math.sqrt(sequences * block * channels)
        second_scale = 1.0 / math.sqrt(sequences * blocks * channels)
        stages = (("near", "x", "far"), ("z", "core"))
        pieces = 1
        for axes in stages:
            pieces *= lax.axis_size(axes)
        first_total = total_of(grad_first.reshape(pieces, -1), stages).reshape(grad_first.shape)
        second_total = total_of((second_one + second_two).reshape(pieces, -1), stages).reshape(block, block)
        return (
            grad_source.reshape(signal.shape),
            grad_gate.reshape(signal.shape),
            grad_kernel,
            first_total * first_scale,
            second_total * second_scale,
        )

    wide = P(dp, seq, None)
    return jax.shard_map(
        body,
        mesh=fine,
        in_specs=(wide, wide, wide, P(None, seq, None), P(), P()),
        out_specs=(wide, wide, wide, P(), P()),
        check_vma=False,
    )
```

```python
import functools
import math

import jax
import jax.numpy as jnp
from jax import lax
from jax.experimental import pallas as pl
from jax.experimental.pallas import tpu as pltpu
from jax.sharding import Mesh, PartitionSpec as P

F32 = jnp.float32
BF16 = jnp.bfloat16
VMEM = pl.BlockSpec(memory_space=pltpu.VMEM)
PARAMS = pltpu.CompilerParams(vmem_limit_bytes=48 * 1024 * 1024)


def halves(value):
    high = value.astype(BF16)
    return high, (value - high.astype(F32)).astype(BF16)


def product(left, right, dims):
    one = lambda a, b: lax.dot_general(a, b, (dims, ((), ())), preferred_element_type=F32)
    return one(left[0], right[0]) + (one(left[0], right[1]) + one(left[1], right[0]))


NN = ((1,), (0,))
TN = ((0,), (0,))
NT = ((1,), (1,))


def enter_kernel(x_ref, s_ref, out_ref):
    rows, block, channels = x_ref.shape
    second = halves(s_ref[...])
    for row in range(rows):
        got = product(second, halves(x_ref[row]), NN)
        out_ref[:, row] = got.reshape(out_ref.shape[0], out_ref.shape[2], channels)


def enter_gated_kernel(g_ref, c_ref, s_ref, out_ref):
    rows, block, channels = g_ref.shape
    second = halves(s_ref[...])
    for row in range(rows):
        got = product(second, halves(g_ref[row] * c_ref[row]), NN)
        out_ref[:, row] = got.reshape(out_ref.shape[0], out_ref.shape[2], channels)


def forward_kernel(a_ref, k_ref, f_ref, z_ref, v_ref):
    first = halves(f_ref[...])
    for k in range(a_ref.shape[1]):
        z = product(first, halves(a_ref[:, k]), NN)
        z_ref[:, k] = z
        v_ref[:, k] = product(first, halves(k_ref[:, k] * z), TN)


def backward_kernel(a_ref, d_ref, k_ref, z_ref, f_ref, da_ref, gk_ref, gf_ref):
    first = halves(f_ref[...])
    total = jnp.zeros(gf_ref.shape, F32)
    for k in range(a_ref.shape[1]):
        dv = halves(d_ref[:, k])
        dw = product(first, dv, NN)
        z = z_ref[:, k]
        weight = k_ref[:, k]
        gk_ref[:, k] = dw * z
        dz = halves(weight * dw)
        da_ref[:, k] = product(first, dz, TN)
        total += product(halves(weight * z), dv, NT) + product(dz, halves(a_ref[:, k]), NT)
    gf_ref[...] = total


def leave_gates_kernel(v_ref, g_ref, c_ref, s_ref, gg_ref, gs_ref):
    rows, block, channels = g_ref.shape
    second = halves(s_ref[...])
    total = jnp.zeros(gs_ref.shape, F32)
    for row in range(rows):
        v = halves(v_ref[:, row].reshape(block, channels))
        gg_ref[row] = c_ref[row] * product(second, v, TN)
        total += product(v, halves(g_ref[row] * c_ref[row]), NT)
    gs_ref[...] = total


def outer_kernel(d_ref, x_ref, gs_ref, gf_ref, out_ref):
    rows, block, channels = x_ref.shape
    pieces, tall, lanes = out_ref.shape
    total = gs_ref[...]
    for row in range(rows):
        d = halves(d_ref[:, row].reshape(block, channels))
        total += product(d, halves(x_ref[row]), NT)
    high = block // pieces
    strips = block // lanes
    for strip in range(strips):
        out_ref[:, strip * high:(strip + 1) * high] = total[:, strip * lanes:(strip + 1) * lanes].reshape(pieces, high, lanes)
    low = gf_ref.shape[0] // pieces
    base = strips * high
    for piece in range(pieces):
        out_ref[piece, base:base + low] = gf_ref[piece * low:(piece + 1) * low]
    out_ref[:, base + low:] = jnp.zeros((pieces, tall - base - low, lanes), F32)


def unpack_kernel(first_scale, second_scale, in_ref, gf_ref, gs_ref):
    pieces, tall, lanes = in_ref.shape
    block = gs_ref.shape[0]
    high = block // pieces
    strips = block // lanes
    for strip in range(strips):
        got = in_ref[:, strip * high:(strip + 1) * high].reshape(block, lanes)
        gs_ref[:, strip * lanes:(strip + 1) * lanes] = got * second_scale
    low = gf_ref.shape[0] // pieces
    base = strips * high
    for piece in range(pieces):
        gf_ref[piece * low:(piece + 1) * low] = in_ref[piece, base:base + low] * first_scale


def leave_signal_kernel(d_ref, s_ref, gx_ref):
    rows, block, channels = gx_ref.shape
    second = halves(s_ref[...])
    for row in range(rows):
        gx_ref[row] = product(second, halves(d_ref[:, row].reshape(block, channels)), TN)


def call(kernel, outs, flops, *args):
    size = sum(math.prod(shape) for shape in outs) + sum(arg.size for arg in args)
    return pl.pallas_call(
        kernel,
        out_shape=[jax.ShapeDtypeStruct(shape, F32) for shape in outs],
        in_specs=[VMEM] * len(args),
        out_specs=[VMEM] * len(outs),
        compiler_params=PARAMS,
        cost_estimate=pl.CostEstimate(flops=flops, bytes_accessed=4 * size, transcendentals=0),
    )(*args)


def exchange(data, axes):
    return lax.all_to_all(data, axes, split_axis=0, concat_axis=0, tiled=True)


def spread(data, axes):
    parts = lax.axis_size(axes)
    return exchange(jnp.broadcast_to(data[None], (parts,) + data.shape), axes)


def swap(data, axis):
    return lax.ppermute(data, axis, [(0, 1), (1, 0)])


def pick(data, axis, index):
    return lax.dynamic_index_in_dim(data, index, axis, keepdims=False)


def halve_sum(data, axis, name):
    me = lax.axis_index(name)
    return pick(data, axis, me) + swap(pick(data, axis, 1 - me), name)


def solution(mesh):
    seq = ("near", "x", "z")
    dp = ("far", "core")
    shape = dict(mesh.shape)
    near = 2
    xs = 4
    fine = Mesh(
        mesh.devices.reshape(near, xs, shape["seq"] // (near * xs), shape["dp"] // 2, 2),
        seq + dp,
    )

    def body(signal, gate_values, cotangent, kernel, first_factor, second_factor):
        blocks = first_factor.shape[0]
        block = second_factor.shape[0]
        channels = signal.shape[2]
        peers = lax.axis_size(seq)
        rows = signal.shape[1] // block
        width = block // peers
        send = (peers, rows, width, channels)
        side = (blocks, width, channels)
        place = (rows, block, channels)
        source = signal.reshape(place)
        gating = gate_values.reshape(place)
        upstream = cotangent.reshape(place)
        second_flops = 6 * rows * block * block * channels
        first_flops = 6 * blocks * blocks * width * channels
        (section,) = call(enter_kernel, [send], second_flops, source, second_factor)
        section = exchange(section, seq).reshape(side)
        (grad_back,) = call(enter_gated_kernel, [send], second_flops, gating, upstream, second_factor)
        grad_back = exchange(grad_back, seq).reshape(side)
        spectrum, back = call(forward_kernel, [side, side], 2 * first_flops, section, kernel, first_factor)
        back = exchange(back.reshape(send), seq)
        grad_section, grad_kernel, grad_first = call(
            backward_kernel,
            [side, side, (blocks, blocks)],
            4 * first_flops,
            section,
            grad_back,
            kernel,
            spectrum,
            first_factor,
        )
        grad_section = exchange(grad_section.reshape(send), seq)
        sequences = lax.axis_size(dp)
        grad_kernel = grad_kernel.reshape(sequences // 2, 2, blocks // sequences, width, channels)
        grad_kernel = halve_sum(halve_sum(grad_kernel, 1, "core"), 0, "far")
        grad_gate, second_part = call(
            leave_gates_kernel,
            [place, (block, block)],
            2 * second_flops,
            back,
            gating,
            upstream,
            second_factor,
        )
        lanes = 128
        across = ("near", "x", "far")
        pieces = 2 * lax.axis_size(across)
        tall = block * block // (lanes * pieces) + -(-blocks // (8 * pieces)) * 8
        (packed,) = call(
            outer_kernel,
            [(pieces, tall, lanes)],
            second_flops,
            grad_section,
            source,
            second_part,
            grad_first,
        )
        (grad_source,) = call(leave_signal_kernel, [place], second_flops, grad_section, second_factor)
        half = halve_sum(packed.reshape(2, pieces // 2, tall, lanes), 0, "core")
        part = jnp.sum(exchange(half, across), axis=0)
        part = jnp.sum(spread(part, "z"), axis=0)
        mine = spread(part, across)
        other = swap(mine, "core")
        me = lax.axis_index("core")
        total = jnp.where(me == 0, jnp.stack([mine, other]), jnp.stack([other, mine]))
        first_scale = 1.0 / math.sqrt(sequences * block * channels)
        second_scale = 1.0 / math.sqrt(sequences * blocks * channels)
        first_total, second_total = call(
            functools.partial(unpack_kernel, first_scale, second_scale),
            [(blocks, blocks), (block, block)],
            0,
            total.reshape(pieces, tall, lanes),
        )
        return (
            grad_source.reshape(signal.shape),
            grad_gate.reshape(signal.shape),
            grad_kernel,
            first_total,
            second_total,
        )

    wide = P(dp, seq, None)
    return jax.shard_map(
        body,
        mesh=fine,
        in_specs=(wide, wide, wide, P(None, seq, None), P(), P()),
        out_specs=(wide, wide, P(dp, seq, None), P(), P()),
        check_vma=False,
    )
```

```python
import functools
import math

import jax
import jax.numpy as jnp
from jax import lax
from jax.experimental import pallas as pl
from jax.experimental.pallas import tpu as pltpu
from jax.sharding import Mesh, PartitionSpec as P

F32 = jnp.float32
BF16 = jnp.bfloat16
VMEM = pl.BlockSpec(memory_space=pltpu.VMEM)
PARAMS = pltpu.CompilerParams(vmem_limit_bytes=24 * 1024 * 1024)


def halves(value):
    high = value.astype(BF16)
    return high, (value - high.astype(F32)).astype(BF16)


def product(left, right, dims):
    one = lambda a, b: lax.dot_general(a, b, (dims, ((), ())), preferred_element_type=F32)
    return one(left[0], right[0]) + (one(left[0], right[1]) + one(left[1], right[0]))


NN = ((1,), (0,))
TN = ((0,), (0,))
NT = ((1,), (1,))


def enter_kernel(x_ref, s_ref, out_ref):
    rows, block, channels = x_ref.shape
    second = halves(s_ref[...])
    for row in range(rows):
        got = product(second, halves(x_ref[row]), NN)
        out_ref[:, row] = got.reshape(out_ref.shape[0], out_ref.shape[2], channels)


def enter_gated_kernel(g_ref, c_ref, s_ref, out_ref):
    rows, block, channels = g_ref.shape
    second = halves(s_ref[...])
    for row in range(rows):
        got = product(second, halves(g_ref[row] * c_ref[row]), NN)
        out_ref[:, row] = got.reshape(out_ref.shape[0], out_ref.shape[2], channels)


def enter(kernel, send, flops, factor, *data):
    rows, block, channels = data[0].shape
    lanes = 128
    size = math.prod(send) + factor.size + sum(each.size for each in data)
    return pl.pallas_call(
        kernel,
        grid=(channels // lanes,),
        out_shape=jax.ShapeDtypeStruct(send, F32),
        in_specs=[pl.BlockSpec((rows, block, lanes), lambda c: (0, 0, c))] * len(data)
        + [pl.BlockSpec(factor.shape, lambda c: (0, 0))],
        out_specs=pl.BlockSpec(send[:3] + (lanes,), lambda c: (0, 0, 0, c)),
        compiler_params=PARAMS,
        cost_estimate=pl.CostEstimate(flops=flops, bytes_accessed=4 * size, transcendentals=0),
    )(*data, factor)


def forward_kernel(a_ref, k_ref, f_ref, z_ref, v_ref):
    first = halves(f_ref[...])
    for k in range(a_ref.shape[1]):
        z = product(first, halves(a_ref[:, k]), NN)
        z_ref[:, k] = z
        v_ref[:, k] = product(first, halves(k_ref[:, k] * z), TN)


def backward_kernel(a_ref, d_ref, k_ref, z_ref, f_ref, da_ref, gk_ref, gf_ref):
    first = halves(f_ref[...])
    blocks = f_ref.shape[0]
    total = jnp.zeros((blocks, blocks), F32)
    for k in range(a_ref.shape[1]):
        dv = halves(d_ref[:, k])
        dw = product(first, dv, NN)
        z = z_ref[:, k]
        weight = k_ref[:, k]
        gk_ref[:, k] = dw * z
        dz = halves(weight * dw)
        da_ref[:, k] = product(first, dz, TN)
        total += product(halves(weight * z), dv, NT) + product(dz, halves(a_ref[:, k]), NT)
    pieces, tall, _ = gf_ref.shape
    low = blocks // pieces
    gf_ref[...] = jnp.zeros(gf_ref.shape, F32)
    for piece in range(pieces):
        gf_ref[piece, :low] = total[piece * low:(piece + 1) * low]


def leave_gates_kernel(v_ref, g_ref, c_ref, s_ref, gg_ref, gs_ref):
    rows, block, channels = g_ref.shape
    second = halves(s_ref[...])
    total = jnp.zeros(gs_ref.shape, F32)
    for row in range(rows):
        v = halves(v_ref[:, row].reshape(block, channels))
        gg_ref[row] = c_ref[row] * product(second, v, TN)
        total += product(v, halves(g_ref[row] * c_ref[row]), NT)
    gs_ref[...] = total


def half_outer(half, d_ref, x_ref, gs_ref, gf_ref, out_ref):
    rows, block, channels = x_ref.shape
    pieces, tall, lanes = out_ref.shape
    peers = d_ref.shape[0] // 2
    total = gs_ref[pl.ds(half * (block // 2), block // 2)]
    for row in range(rows):
        d = halves(d_ref[pl.ds(half * peers, peers), row].reshape(block // 2, channels))
        total += product(d, halves(x_ref[row]), NT)
    high = block // (2 * pieces)
    strips = block // lanes
    return [
        (slice(strip * high, (strip + 1) * high), total[:, strip * lanes:(strip + 1) * lanes].reshape(pieces, high, lanes))
        for strip in range(strips)
    ] + [(slice(strips * high, tall), gf_ref[pl.ds(half * pieces, pieces)])]


def send_kernel(me_ref, d_ref, x_ref, gs_ref, gf_ref, after_ref, out_ref):
    for rows, value in half_outer(1 - me_ref[0], d_ref, x_ref, gs_ref, gf_ref, out_ref):
        out_ref[:, rows] = value


def keep_kernel(me_ref, d_ref, x_ref, gs_ref, gf_ref, got_ref, out_ref):
    for rows, value in half_outer(me_ref[0], d_ref, x_ref, gs_ref, gf_ref, out_ref):
        out_ref[:, rows] = value + got_ref[:, rows]


def sum_kernel(in_ref, after_ref, out_ref):
    total = in_ref[0]
    for part in range(1, in_ref.shape[0]):
        total += in_ref[part]
    out_ref[...] = jnp.broadcast_to(total[None], out_ref.shape)


def unpack_kernel(first_scale, second_scale, me_ref, mine_ref, other_ref, gf_ref, gs_ref):
    pieces, tall, lanes = mine_ref.shape
    block = gs_ref.shape[0]
    high = block // (2 * pieces)
    strips = block // lanes
    me = me_ref[0]
    for half, ref in ((me, mine_ref), (1 - me, other_ref)):
        rows = pl.ds(pl.multiple_of(half * (block // 2), block // 2), block // 2)
        for strip in range(strips):
            got = ref[:, strip * high:(strip + 1) * high].reshape(block // 2, lanes)
            gs_ref[rows, strip * lanes:(strip + 1) * lanes] = got * second_scale
    low = gf_ref.shape[0] // (2 * pieces)
    base = strips * high
    for piece in range(pieces):
        mine = mine_ref[piece, base:base + low] * first_scale
        other = other_ref[piece, base:base + low] * first_scale
        gf_ref[piece * low:(piece + 1) * low] = jnp.where(me == 0, mine, other)
        gf_ref[(piece + pieces) * low:(piece + pieces + 1) * low] = jnp.where(me == 0, other, mine)


def leave_signal_kernel(d_ref, s_ref, gx_ref, token_ref):
    token_ref[...] = jnp.zeros(token_ref.shape, F32)
    rows, block, channels = gx_ref.shape
    second = halves(s_ref[...])
    for row in range(rows):
        gx_ref[row] = product(second, halves(d_ref[:, row].reshape(block, channels)), TN)


SCALAR = pl.BlockSpec(memory_space=pltpu.SMEM)
UNREAD = pl.BlockSpec(memory_space=pl.ANY)


def call(kernel, outs, flops, *args, specs=None):
    size = sum(math.prod(shape) for shape in outs) + sum(arg.size for arg in args)
    return pl.pallas_call(
        kernel,
        out_shape=[jax.ShapeDtypeStruct(shape, F32) for shape in outs],
        in_specs=specs or [VMEM] * len(args),
        out_specs=[VMEM] * len(outs),
        compiler_params=PARAMS,
        cost_estimate=pl.CostEstimate(flops=flops, bytes_accessed=4 * size, transcendentals=0),
    )(*args)


def exchange(data, axes):
    return lax.all_to_all(data, axes, split_axis=0, concat_axis=0, tiled=True)


def swap(data, axis):
    return lax.ppermute(data, axis, [(0, 1), (1, 0)])


def pick(data, axis, index):
    return lax.dynamic_index_in_dim(data, index, axis, keepdims=False)


def halve_sum(data, axis, name):
    me = lax.axis_index(name)
    return pick(data, axis, me) + swap(pick(data, axis, 1 - me), name)


def solution(mesh):
    seq = ("near", "x", "z")
    dp = ("far", "core")
    shape = dict(mesh.shape)
    near = 2
    xs = 4
    fine = Mesh(
        mesh.devices.reshape(near, xs, shape["seq"] // (near * xs), shape["dp"] // 2, 2),
        seq + dp,
    )

    def body(signal, gate_values, cotangent, kernel, first_factor, second_factor):
        blocks = first_factor.shape[0]
        block = second_factor.shape[0]
        channels = signal.shape[2]
        peers = lax.axis_size(seq)
        rows = signal.shape[1] // block
        width = block // peers
        send = (peers, rows, width, channels)
        side = (blocks, width, channels)
        place = (rows, block, channels)
        source = signal.reshape(place)
        gating = gate_values.reshape(place)
        upstream = cotangent.reshape(place)
        second_flops = 6 * rows * block * block * channels
        first_flops = 6 * blocks * blocks * width * channels
        section = enter(enter_kernel, send, second_flops, second_factor, source)
        lanes = 128
        across = ("near", "x", "far")
        pieces = lax.axis_size(across)
        low = -(-blocks // (16 * pieces)) * 8
        tall = block * block // (2 * lanes * pieces) + low
        section = exchange(section, seq).reshape(side)
        grad_back = enter(enter_gated_kernel, send, second_flops, second_factor, gating, upstream)
        grad_back = exchange(grad_back, seq).reshape(side)
        spectrum, back = call(forward_kernel, [side, side], 2 * first_flops, section, kernel, first_factor)
        back = exchange(back.reshape(send), seq)
        grad_section, grad_kernel, grad_first = call(
            backward_kernel,
            [side, side, (2 * pieces, low, lanes)],
            4 * first_flops,
            section,
            grad_back,
            kernel,
            spectrum,
            first_factor,
        )
        grad_section = exchange(grad_section.reshape(send), seq)
        sequences = lax.axis_size(dp)
        grad_kernel = grad_kernel.reshape(sequences // 2, 2, blocks // sequences, width, channels)
        grad_kernel = halve_sum(halve_sum(grad_kernel, 1, "core"), 0, "far")
        grad_gate, second_part = call(
            leave_gates_kernel,
            [place, (block, block)],
            2 * second_flops,
            back,
            gating,
            upstream,
            second_factor,
        )
        me = lax.axis_index("core").reshape(1)
        packet = (pieces, tall, lanes)
        outer_args = (me, grad_section, source, second_part, grad_first)
        (half,) = call(
            send_kernel, [packet], second_flops // 2, *outer_args, grad_kernel[:1], specs=[SCALAR] + [VMEM] * 4 + [UNREAD]
        )
        half = swap(half, "core")
        (half,) = call(keep_kernel, [packet], second_flops // 2, *outer_args, half, specs=[SCALAR] + [VMEM] * 5)
        grad_source, token = call(leave_signal_kernel, [place, (8, lanes)], second_flops, grad_section, second_factor)
        deep = lax.axis_size("z")
        (part,) = call(sum_kernel, [(deep, tall, lanes)], 0, exchange(half, across), token, specs=[VMEM, UNREAD])
        part = exchange(part, "z")
        (part,) = call(sum_kernel, [packet], 0, part, token, specs=[VMEM, UNREAD])
        mine = exchange(part, across)
        other = swap(mine, "core")
        first_scale = 1.0 / math.sqrt(sequences * block * channels)
        second_scale = 1.0 / math.sqrt(sequences * blocks * channels)
        first_total, second_total = call(
            functools.partial(unpack_kernel, first_scale, second_scale),
            [(blocks, blocks), (block, block)],
            0,
            me,
            mine,
            other,
            specs=[SCALAR, VMEM, VMEM],
        )
        return (
            grad_source.reshape(signal.shape),
            grad_gate.reshape(signal.shape),
            grad_kernel,
            first_total,
            second_total,
        )

    wide = P(dp, seq, None)
    return jax.shard_map(
        body,
        mesh=fine,
        in_specs=(wide, wide, wide, P(None, seq, None), P(), P()),
        out_specs=(wide, wide, P(dp, seq, None), P(), P()),
        check_vma=False,
    )
```

```python
import functools
import math

import jax
import jax.numpy as jnp
from jax import lax
from jax.experimental import pallas as pl
from jax.experimental.pallas import tpu as pltpu
from jax.sharding import Mesh, PartitionSpec as P

F32 = jnp.float32
BF16 = jnp.bfloat16
VMEM = pl.BlockSpec(memory_space=pltpu.VMEM)
PARAMS = pltpu.CompilerParams(vmem_limit_bytes=24 * 1024 * 1024)


def halves(value):
    high = value.astype(BF16)
    return high, (value - high.astype(F32)).astype(BF16)


def product(left, right, dims):
    one = lambda a, b: lax.dot_general(a, b, (dims, ((), ())), preferred_element_type=F32)
    return one(left[0], right[0]) + (one(left[0], right[1]) + one(left[1], right[0]))


NN = ((1,), (0,))
TN = ((0,), (0,))
NT = ((1,), (1,))


def enter_kernel(count, *refs):
    data, second_ref, out_ref = refs[:count], refs[count], refs[count + 1]
    held, s_ref, made = refs[count + 2:2 * count + 2], refs[2 * count + 2], refs[2 * count + 3]
    data_sem, s_sem, out_sem = refs[2 * count + 4:]
    deep, xs, near, rows, width, channels = out_ref.shape
    half = s_ref.shape[0] // near

    def fetch(row):
        return [
            pltpu.make_async_copy(data[n].at[row], held[n].at[row], data_sem.at[n, row]) for n in range(count)
        ]

    fetches = [fetch(row) for row in range(rows)]
    factors = [
        pltpu.make_async_copy(second_ref.at[pl.ds(n * half, half)], s_ref.at[pl.ds(n * half, half)], s_sem.at[n])
        for n in range(near)
    ]
    for copy in fetches[0] + factors + [copy for row in fetches[1:] for copy in row]:
        copy.start()
    seconds = []
    sends = []
    for row in range(rows):
        for copy in fetches[row]:
            copy.wait()
        value = held[0][row]
        for ref in held[1:]:
            value = value * ref[row]
        value = halves(value)
        for n in range(near):
            if row == 0:
                factors[n].wait()
                seconds.append(halves(s_ref[n * half:(n + 1) * half]))
            got = product(seconds[n], value, NN)
            made[n, :, :, row] = got.reshape(xs, deep, width, channels)
            for x in range(xs):
                copy = pltpu.make_async_copy(made.at[n, x, :, row], out_ref.at[:, x, n, row], out_sem.at[row, n, x])
                copy.start()
                sends.append(copy)
    for copy in sends:
        copy.wait()


def enter(send, flops, factor, *data):
    count = len(data)
    deep, xs, near, rows, width, channels = send
    size = math.prod(send) + factor.size + sum(each.size for each in data)
    return pl.pallas_call(
        functools.partial(enter_kernel, count),
        out_shape=jax.ShapeDtypeStruct(send, F32),
        in_specs=[FAR] * (count + 1),
        out_specs=FAR,
        scratch_shapes=[pltpu.VMEM(each.shape, F32) for each in data]
        + [
            pltpu.VMEM(factor.shape, F32),
            pltpu.VMEM((near, xs, deep, rows, width, channels), F32),
            pltpu.SemaphoreType.DMA((count, rows)),
            pltpu.SemaphoreType.DMA((near,)),
            pltpu.SemaphoreType.DMA((rows, near, xs)),
        ],
        compiler_params=PARAMS,
        cost_estimate=pl.CostEstimate(flops=flops, bytes_accessed=4 * size, transcendentals=0),
    )(*data, factor)


def lines(ref, row, nears):
    deep, xs, near, rows, width, channels = ref.shape
    return jnp.concatenate([ref[:, x, n, row].reshape(deep * width, channels) for n in nears for x in range(xs)], axis=0)


def forward_kernel(a_ref, k_ref, f_ref, z_ref, v_ref):
    first = halves(f_ref[...])
    for k in range(a_ref.shape[1]):
        z = product(first, halves(a_ref[:, k]), NN)
        z_ref[:, k] = z
        v_ref[:, k] = product(first, halves(k_ref[:, k] * z), TN)


def backward_kernel(a_ref, d_ref, k_ref, z_ref, f_ref, da_ref, gk_ref, gf_ref):
    first = halves(f_ref[...])
    total = jnp.zeros(gf_ref.shape, F32)
    for k in range(a_ref.shape[1]):
        dv = halves(d_ref[:, k])
        dw = product(first, dv, NN)
        z = z_ref[:, k]
        weight = k_ref[:, k]
        gk_ref[:, k] = dw * z
        dz = halves(weight * dw)
        da_ref[:, k] = product(first, dz, TN)
        total += product(halves(weight * z), dv, NT) + product(dz, halves(a_ref[:, k]), NT)
    gf_ref[...] = total


def leave_gates_kernel(v_ref, g_ref, c_ref, s_ref, gg_ref, gs_ref):
    rows, block, channels = g_ref.shape
    second = halves(s_ref[...])
    total = jnp.zeros(gs_ref.shape, F32)
    for row in range(rows):
        v = halves(lines(v_ref, row, range(v_ref.shape[2])))
        gg_ref[row] = c_ref[row] * product(second, v, TN)
        total += product(v, halves(g_ref[row] * c_ref[row]), NT)
    gs_ref[...] = total


def half_outer(half, d_ref, x_ref, gs_ref, gf_ref, part, sem, packet):
    rows, block, channels = x_ref.shape
    pieces, tall, lanes = packet
    fetch = pltpu.make_async_copy(gs_ref.at[pl.ds(pl.multiple_of(half * (block // 2), block // 2), block // 2)], part, sem)
    fetch.start()
    total = jnp.zeros(part.shape, F32)
    for row in range(rows):
        total += product(halves(lines(d_ref, row, [half])), halves(x_ref[row]), NT)
    fetch.wait()
    total += part[...]
    high = block // (2 * pieces)
    strips = block // lanes
    return [
        (slice(strip * high, (strip + 1) * high), total[:, strip * lanes:(strip + 1) * lanes].reshape(pieces, high, lanes))
        for strip in range(strips)
    ] + [(slice(strips * high, tall), gf_ref[pl.ds(half * pieces, pieces)])]


def send_kernel(me_ref, d_ref, x_ref, gs_ref, gf_ref, after_ref, out_ref, part, sem):
    for rows, value in half_outer(1 - me_ref[0], d_ref, x_ref, gs_ref, gf_ref, part, sem, out_ref.shape):
        out_ref[:, rows] = value


def keep_kernel(me_ref, d_ref, x_ref, gs_ref, gf_ref, got_ref, out_ref, part, sem):
    for rows, value in half_outer(me_ref[0], d_ref, x_ref, gs_ref, gf_ref, part, sem, out_ref.shape):
        out_ref[:, rows] = value + got_ref[:, rows]


def sum_kernel(in_ref, after_ref, out_ref):
    total = in_ref[0]
    for part in range(1, in_ref.shape[0]):
        total += in_ref[part]
    out_ref[...] = jnp.broadcast_to(total[None], out_ref.shape)


def unpack_kernel(first_scale, second_scale, me_ref, mine_ref, other_ref, gf_ref, gs_ref):
    pieces, tall, lanes = mine_ref.shape
    block = gs_ref.shape[0]
    high = block // (2 * pieces)
    strips = block // lanes
    me = me_ref[0]
    for half, ref in ((me, mine_ref), (1 - me, other_ref)):
        rows = pl.ds(pl.multiple_of(half * (block // 2), block // 2), block // 2)
        for strip in range(strips):
            got = ref[:, strip * high:(strip + 1) * high].reshape(block // 2, lanes)
            gs_ref[rows, strip * lanes:(strip + 1) * lanes] = got * second_scale
    low = gf_ref.shape[0] // (2 * pieces)
    base = strips * high
    for piece in range(pieces):
        mine = mine_ref[piece, base:base + low] * first_scale
        other = other_ref[piece, base:base + low] * first_scale
        gf_ref[piece * low:(piece + 1) * low] = jnp.where(me == 0, mine, other)
        gf_ref[(piece + pieces) * low:(piece + pieces + 1) * low] = jnp.where(me == 0, other, mine)


def leave_signal_kernel(d_ref, s_ref, gx_ref, token_ref):
    token_ref[...] = jnp.zeros(token_ref.shape, F32)
    rows, block, channels = gx_ref.shape
    second = halves(s_ref[...])
    for row in range(rows):
        gx_ref[row] = product(second, halves(lines(d_ref, row, range(d_ref.shape[2]))), TN)


SCALAR = pl.BlockSpec(memory_space=pltpu.SMEM)
UNREAD = pl.BlockSpec(memory_space=pl.ANY)
FAR = pl.BlockSpec(memory_space=pltpu.HBM)


def call(kernel, outs, flops, *args, specs=None, scratch=()):
    size = sum(math.prod(shape) for shape in outs) + sum(arg.size for arg in args)
    return pl.pallas_call(
        kernel,
        out_shape=[jax.ShapeDtypeStruct(shape, F32) for shape in outs],
        in_specs=specs or [VMEM] * len(args),
        out_specs=[VMEM] * len(outs),
        scratch_shapes=list(scratch),
        compiler_params=PARAMS,
        cost_estimate=pl.CostEstimate(flops=flops, bytes_accessed=4 * size, transcendentals=0),
    )(*args)


def exchange(data, axes):
    return lax.all_to_all(data, axes, split_axis=0, concat_axis=0, tiled=True)


def swap(data, axis):
    return lax.ppermute(data, axis, [(0, 1), (1, 0)])


def pick(data, axis, index):
    return lax.dynamic_index_in_dim(data, index, axis, keepdims=False)


def halve_sum(data, axis, name):
    me = lax.axis_index(name)
    return pick(data, axis, me) + swap(pick(data, axis, 1 - me), name)


def solution(mesh):
    seq = ("near", "x", "z")
    order = ("z", "x", "near")
    dp = ("far", "core")
    shape = dict(mesh.shape)
    near = 2
    xs = 4
    fine = Mesh(
        mesh.devices.reshape(near, xs, shape["seq"] // (near * xs), shape["dp"] // 2, 2),
        seq + dp,
    )

    def body(signal, gate_values, cotangent, kernel, first_factor, second_factor):
        blocks = first_factor.shape[0]
        block = second_factor.shape[0]
        channels = signal.shape[2]
        peers = lax.axis_size(seq)
        rows = signal.shape[1] // block
        width = block // peers
        near, xs, deep = (lax.axis_size(name) for name in seq)
        send = (deep, xs, near, rows, width, channels)
        flat = (peers, rows, width, channels)
        side = (blocks, width, channels)
        place = (rows, block, channels)
        source = signal.reshape(place)
        gating = gate_values.reshape(place)
        upstream = cotangent.reshape(place)
        second_flops = 6 * rows * block * block * channels
        first_flops = 6 * blocks * blocks * width * channels
        turned = first_factor.reshape(blocks, near, xs, deep, rows).transpose(0, 3, 2, 1, 4).reshape(blocks, blocks)
        section = enter(send, second_flops, second_factor, source)
        lanes = 128
        across = ("near", "x", "far")
        pieces = lax.axis_size(across)
        low = -(-blocks // (16 * pieces)) * 8
        tall = block * block // (2 * lanes * pieces) + low
        section = exchange(section.reshape(flat), order).reshape(side)
        grad_back = enter(send, second_flops, second_factor, gating, upstream)
        grad_back = exchange(grad_back.reshape(flat), order).reshape(side)
        spectrum, back = call(forward_kernel, [side, side], 2 * first_flops, section, kernel, turned)
        back = exchange(back.reshape(flat), order).reshape(send)
        grad_section, grad_kernel, grad_first = call(
            backward_kernel,
            [side, side, (blocks, blocks)],
            4 * first_flops,
            section,
            grad_back,
            kernel,
            spectrum,
            turned,
        )
        grad_section = exchange(grad_section.reshape(flat), order).reshape(send)
        grad_first = grad_first.reshape(blocks, deep, xs, near, rows).transpose(0, 3, 2, 1, 4)
        grad_first = grad_first.reshape(2 * pieces, blocks // (2 * pieces), blocks)
        grad_first = jnp.pad(grad_first, ((0, 0), (0, low - grad_first.shape[1]), (0, 0)))
        sequences = lax.axis_size(dp)
        grad_kernel = grad_kernel.reshape(sequences // 2, 2, blocks // sequences, width, channels)
        grad_kernel = halve_sum(halve_sum(grad_kernel, 1, "core"), 0, "far")
        grad_gate, second_part = call(
            leave_gates_kernel,
            [place, (block, block)],
            2 * second_flops,
            back,
            gating,
            upstream,
            second_factor,
        )
        me = lax.axis_index("core").reshape(1)
        packet = (pieces, tall, lanes)
        outer_args = (me, grad_section, source, second_part, grad_first)
        outer_specs = [SCALAR, VMEM, VMEM, FAR, VMEM]
        scratch = [pltpu.VMEM((block // 2, block), F32), pltpu.SemaphoreType.DMA]
        (half,) = call(
            send_kernel,
            [packet],
            second_flops // 2,
            *outer_args,
            grad_kernel[:1],
            specs=outer_specs + [UNREAD],
            scratch=scratch,
        )
        half = swap(half, "core")
        (half,) = call(
            keep_kernel, [packet], second_flops // 2, *outer_args, half, specs=outer_specs + [VMEM], scratch=scratch
        )
        grad_source, token = call(leave_signal_kernel, [place, (8, lanes)], second_flops, grad_section, second_factor)
        (part,) = call(sum_kernel, [(deep, tall, lanes)], 0, exchange(half, across), token, specs=[VMEM, UNREAD])
        part = exchange(part, "z")
        (part,) = call(sum_kernel, [packet], 0, part, token, specs=[VMEM, UNREAD])
        mine = exchange(part, across)
        other = swap(mine, "core")
        first_scale = 1.0 / math.sqrt(sequences * block * channels)
        second_scale = 1.0 / math.sqrt(sequences * blocks * channels)
        first_total, second_total = call(
            functools.partial(unpack_kernel, first_scale, second_scale),
            [(blocks, blocks), (block, block)],
            0,
            me,
            mine,
            other,
            specs=[SCALAR, VMEM, VMEM],
        )
        return (
            grad_source.reshape(signal.shape),
            grad_gate.reshape(signal.shape),
            grad_kernel,
            first_total,
            second_total,
        )

    wide = P(dp, seq, None)
    return jax.shard_map(
        body,
        mesh=fine,
        in_specs=(wide, wide, wide, P(None, seq, None), P(), P()),
        out_specs=(wide, wide, P(dp, seq, None), P(), P()),
        check_vma=False,
    )
```

```python
import functools
import math

import jax
import jax.numpy as jnp
from jax import lax
from jax.experimental import pallas as pl
from jax.experimental.pallas import tpu as pltpu
from jax.sharding import Mesh, PartitionSpec as P

F32 = jnp.float32
BF16 = jnp.bfloat16
VMEM = pl.BlockSpec(memory_space=pltpu.VMEM)
PARAMS = pltpu.CompilerParams(vmem_limit_bytes=24 * 1024 * 1024)


def halves(value):
    high = value.astype(BF16)
    return high, (value - high.astype(F32)).astype(BF16)


def product(left, right, dims):
    one = lambda a, b: lax.dot_general(a, b, (dims, ((), ())), preferred_element_type=F32)
    return one(left[0], right[0]) + (one(left[0], right[1]) + one(left[1], right[0]))


NN = ((1,), (0,))
TN = ((0,), (0,))
NT = ((1,), (1,))


def enter_kernel(count, *refs):
    data, second_ref, out_ref = refs[:count], refs[count], refs[count + 2]
    held, s_ref, made = refs[count + 3:2 * count + 3], refs[2 * count + 3], refs[2 * count + 4]
    data_sem, s_sem, out_sem = refs[2 * count + 5:]
    deep, xs, near, rows, width, channels = out_ref.shape
    half = s_ref.shape[0] // near

    def fetch(row):
        return [
            pltpu.make_async_copy(data[n].at[row], held[n].at[row], data_sem.at[n, row]) for n in range(count)
        ]

    fetches = [fetch(row) for row in range(rows)]
    factors = [
        pltpu.make_async_copy(second_ref.at[pl.ds(n * half, half)], s_ref.at[pl.ds(n * half, half)], s_sem.at[n])
        for n in range(near)
    ]
    for copy in fetches[0] + factors + [copy for row in fetches[1:] for copy in row]:
        copy.start()
    seconds = []
    sends = []
    for row in range(rows):
        for copy in fetches[row]:
            copy.wait()
        value = held[0][row]
        for ref in held[1:]:
            value = value * ref[row]
        value = halves(value)
        for n in range(near):
            if row == 0:
                factors[n].wait()
                seconds.append(halves(s_ref[n * half:(n + 1) * half]))
            got = product(seconds[n], value, NN)
            made[n, :, :, row] = got.reshape(xs, deep, width, channels)
            for x in range(xs):
                copy = pltpu.make_async_copy(made.at[n, x, :, row], out_ref.at[:, x, n, row], out_sem.at[row, n, x])
                copy.start()
                sends.append(copy)
    for copy in sends:
        copy.wait()


def enter(send, flops, factor, after, *data):
    count = len(data)
    deep, xs, near, rows, width, channels = send
    size = math.prod(send) + factor.size + sum(each.size for each in data)
    return pl.pallas_call(
        functools.partial(enter_kernel, count),
        out_shape=jax.ShapeDtypeStruct(send, F32),
        in_specs=[FAR] * (count + 1) + [UNREAD],
        out_specs=FAR,
        scratch_shapes=[pltpu.VMEM(each.shape, F32) for each in data]
        + [
            pltpu.VMEM(factor.shape, F32),
            pltpu.VMEM((near, xs, deep, rows, width, channels), F32),
            pltpu.SemaphoreType.DMA((count, rows)),
            pltpu.SemaphoreType.DMA((near,)),
            pltpu.SemaphoreType.DMA((rows, near, xs)),
        ],
        compiler_params=PARAMS,
        cost_estimate=pl.CostEstimate(flops=flops, bytes_accessed=4 * size, transcendentals=0),
    )(*data, factor, after)


def lines(ref, row, nears):
    deep, xs, near, rows, width, channels = ref.shape
    return jnp.concatenate([ref[:, x, n, row].reshape(deep * width, channels) for n in nears for x in range(xs)], axis=0)


def forward_kernel(a_ref, k_ref, f_ref, z_ref, v_ref):
    first = halves(f_ref[...])
    for k in range(a_ref.shape[1]):
        z = product(first, halves(a_ref[:, k]), NN)
        z_ref[:, k] = z
        v_ref[:, k] = product(first, halves(k_ref[:, k] * z), TN)


def backward_kernel(shape, a_ref, d_ref, k_ref, z_ref, f_ref, da_ref, gk_ref, gf_ref, lines_ref):
    first = halves(f_ref[...])
    total = jnp.zeros(lines_ref.shape, F32)
    for k in range(a_ref.shape[1]):
        dv = halves(d_ref[:, k])
        dw = product(first, dv, NN)
        z = z_ref[:, k]
        weight = k_ref[:, k]
        gk_ref[:, k] = dw * z
        dz = halves(weight * dw)
        da_ref[:, k] = product(first, dz, TN)
        total += product(dv, halves(weight * z), NT) + product(halves(a_ref[:, k]), dz, NT)
    deep, xs, near, rows = shape
    for z in range(deep):
        for x in range(xs):
            for n in range(near):
                at = ((z * xs + x) * near + n) * rows
                to = ((n * xs + x) * deep + z) * rows
                lines_ref[to:to + rows] = total[at:at + rows]
    turned = lines_ref[...].T
    pieces, tall, lanes = gf_ref.shape
    low = turned.shape[0] // pieces
    gf_ref[...] = jnp.zeros(gf_ref.shape, F32)
    for piece in range(pieces):
        gf_ref[piece, :low] = turned[piece * low:(piece + 1) * low]


def leave_gates_kernel(v_ref, g_ref, c_ref, s_ref, gk_ref, gg_ref, gs_ref, same_ref):
    rows, block, channels = g_ref.shape
    second = halves(s_ref[...])
    total = jnp.zeros(gs_ref.shape, F32)
    for row in range(rows):
        v = halves(lines(v_ref, row, range(v_ref.shape[2])))
        gg_ref[row] = c_ref[row] * product(second, v, TN)
        total += product(v, halves(g_ref[row] * c_ref[row]), NT)
    gs_ref[...] = total


def half_outer(half, d_ref, x_ref, gs_ref, gf_ref, part, sem, packet):
    rows, block, channels = x_ref.shape
    pieces, tall, lanes = packet
    fetch = pltpu.make_async_copy(gs_ref.at[pl.ds(pl.multiple_of(half * (block // 2), block // 2), block // 2)], part, sem)
    fetch.start()
    total = jnp.zeros(part.shape, F32)
    for row in range(rows):
        total += product(halves(lines(d_ref, row, [half])), halves(x_ref[row]), NT)
    fetch.wait()
    total += part[...]
    high = block // (2 * pieces)
    strips = block // lanes
    return [
        (slice(strip * high, (strip + 1) * high), total[:, strip * lanes:(strip + 1) * lanes].reshape(pieces, high, lanes))
        for strip in range(strips)
    ] + [(slice(strips * high, tall), gf_ref[pl.ds(half * pieces, pieces)])]


def send_kernel(me_ref, d_ref, x_ref, gs_ref, gf_ref, after_ref, out_ref, part, sem):
    for rows, value in half_outer(1 - me_ref[0], d_ref, x_ref, gs_ref, gf_ref, part, sem, out_ref.shape):
        out_ref[:, rows] = value


def keep_kernel(me_ref, d_ref, x_ref, gs_ref, gf_ref, got_ref, out_ref, part, sem):
    for rows, value in half_outer(me_ref[0], d_ref, x_ref, gs_ref, gf_ref, part, sem, out_ref.shape):
        out_ref[:, rows] = value + got_ref[:, rows]


def sum_kernel(in_ref, after_ref, out_ref):
    total = in_ref[0]
    for part in range(1, in_ref.shape[0]):
        total += in_ref[part]
    out_ref[...] = jnp.broadcast_to(total[None], out_ref.shape)


def unpack_kernel(first_scale, second_scale, me_ref, mine_ref, other_ref, gf_ref, gs_ref):
    pieces, tall, lanes = mine_ref.shape
    block = gs_ref.shape[0]
    high = block // (2 * pieces)
    strips = block // lanes
    me = me_ref[0]
    for half, ref in ((me, mine_ref), (1 - me, other_ref)):
        rows = pl.ds(pl.multiple_of(half * (block // 2), block // 2), block // 2)
        for strip in range(strips):
            got = ref[:, strip * high:(strip + 1) * high].reshape(block // 2, lanes)
            gs_ref[rows, strip * lanes:(strip + 1) * lanes] = got * second_scale
    low = gf_ref.shape[0] // (2 * pieces)
    base = strips * high
    for piece in range(pieces):
        mine = mine_ref[piece, base:base + low] * first_scale
        other = other_ref[piece, base:base + low] * first_scale
        gf_ref[piece * low:(piece + 1) * low] = jnp.where(me == 0, mine, other)
        gf_ref[(piece + pieces) * low:(piece + pieces + 1) * low] = jnp.where(me == 0, other, mine)


def leave_signal_kernel(d_ref, s_ref, gx_ref, token_ref):
    token_ref[...] = jnp.zeros(token_ref.shape, F32)
    rows, block, channels = gx_ref.shape
    second = halves(s_ref[...])
    for row in range(rows):
        gx_ref[row] = product(second, halves(lines(d_ref, row, range(d_ref.shape[2]))), TN)


SCALAR = pl.BlockSpec(memory_space=pltpu.SMEM)
UNREAD = pl.BlockSpec(memory_space=pl.ANY)
FAR = pl.BlockSpec(memory_space=pltpu.HBM)


def call(kernel, outs, flops, *args, specs=None, out_specs=None, aliases=None, scratch=()):
    size = sum(math.prod(shape) for shape in outs) + sum(arg.size for arg in args)
    return pl.pallas_call(
        kernel,
        out_shape=[jax.ShapeDtypeStruct(shape, F32) for shape in outs],
        in_specs=specs or [VMEM] * len(args),
        out_specs=out_specs or [VMEM] * len(outs),
        input_output_aliases=aliases or {},
        scratch_shapes=list(scratch),
        compiler_params=PARAMS,
        cost_estimate=pl.CostEstimate(flops=flops, bytes_accessed=4 * size, transcendentals=0),
    )(*args)


def exchange(data, axes):
    return lax.all_to_all(data, axes, split_axis=0, concat_axis=0, tiled=True)


def swap(data, axis):
    return lax.ppermute(data, axis, [(0, 1), (1, 0)])


def pick(data, axis, index):
    return lax.dynamic_index_in_dim(data, index, axis, keepdims=False)


def halve_sum(data, axis, name):
    me = lax.axis_index(name)
    return pick(data, axis, me) + swap(pick(data, axis, 1 - me), name)


def solution(mesh):
    seq = ("near", "x", "z")
    order = ("z", "x", "near")
    dp = ("far", "core")
    shape = dict(mesh.shape)
    near = 2
    xs = 4
    fine = Mesh(
        mesh.devices.reshape(near, xs, shape["seq"] // (near * xs), shape["dp"] // 2, 2),
        seq + dp,
    )

    def body(signal, gate_values, cotangent, kernel, first_factor, second_factor):
        blocks = first_factor.shape[0]
        block = second_factor.shape[0]
        channels = signal.shape[2]
        peers = lax.axis_size(seq)
        rows = signal.shape[1] // block
        width = block // peers
        near, xs, deep = (lax.axis_size(name) for name in seq)
        send = (deep, xs, near, rows, width, channels)
        flat = (peers, rows, width, channels)
        side = (blocks, width, channels)
        place = (rows, block, channels)
        source = signal.reshape(place)
        gating = gate_values.reshape(place)
        upstream = cotangent.reshape(place)
        second_flops = 6 * rows * block * block * channels
        first_flops = 6 * blocks * blocks * width * channels
        turned = first_factor.reshape(blocks, near, xs, deep, rows).transpose(0, 3, 2, 1, 4).reshape(blocks, blocks)
        turn = first_factor[:8]
        for _ in range(4):
            turn = lax.ppermute(turn, ("x", "core"), [(2 * x + 1, (2 * x + 3) % (2 * xs)) for x in range(xs)])
        section = enter(send, second_flops, second_factor, turn, source)
        lanes = 128
        across = ("near", "x", "far")
        pieces = lax.axis_size(across)
        low = -(-blocks // (16 * pieces)) * 8
        tall = block * block // (2 * lanes * pieces) + low
        section = exchange(section.reshape(flat), order).reshape(side)
        grad_back = enter(send, second_flops, second_factor, turn, gating, upstream)
        grad_back = exchange(grad_back.reshape(flat), order).reshape(side)
        spectrum, back = call(forward_kernel, [side, side], 2 * first_flops, section, kernel, turned)
        back = exchange(back.reshape(flat), order).reshape(send)
        grad_section, grad_kernel, grad_first = call(
            functools.partial(backward_kernel, (deep, xs, near, rows)),
            [side, side, (2 * pieces, low, lanes)],
            4 * first_flops,
            section,
            grad_back,
            kernel,
            spectrum,
            turned,
            scratch=[pltpu.VMEM((blocks, blocks), F32)],
        )
        grad_section = exchange(grad_section.reshape(flat), order).reshape(send)
        grad_gate, second_part, grad_kernel = call(
            leave_gates_kernel,
            [place, (block, block), side],
            2 * second_flops,
            back,
            gating,
            upstream,
            second_factor,
            grad_kernel,
            specs=[VMEM] * 4 + [UNREAD],
            out_specs=[VMEM] * 2 + [UNREAD],
            aliases={4: 2},
        )
        sequences = lax.axis_size(dp)
        grad_kernel = grad_kernel.reshape(sequences // 2, 2, blocks // sequences, width, channels)
        kernel_pair = halve_sum(grad_kernel, 1, "core")
        grad_kernel = halve_sum(kernel_pair, 0, "far")
        me = lax.axis_index("core").reshape(1)
        packet = (pieces, tall, lanes)
        outer_args = (me, grad_section, source, second_part, grad_first)
        outer_specs = [SCALAR, VMEM, VMEM, FAR, VMEM]
        scratch = [pltpu.VMEM((block // 2, block), F32), pltpu.SemaphoreType.DMA]
        (half,) = call(
            send_kernel,
            [packet],
            second_flops // 2,
            *outer_args,
            kernel_pair[0, :1],
            specs=outer_specs + [UNREAD],
            scratch=scratch,
        )
        half = swap(half, "core")
        (half,) = call(
            keep_kernel, [packet], second_flops // 2, *outer_args, half, specs=outer_specs + [VMEM], scratch=scratch
        )
        grad_source, token = call(leave_signal_kernel, [place, (8, lanes)], second_flops, grad_section, second_factor)
        (part,) = call(sum_kernel, [(deep, tall, lanes)], 0, exchange(half, across), token, specs=[VMEM, UNREAD])
        part = exchange(part, "z")
        (part,) = call(sum_kernel, [packet], 0, part, grad_kernel[:1], specs=[VMEM, UNREAD])
        mine = exchange(part, across)
        other = swap(mine, "core")
        first_scale = 1.0 / math.sqrt(sequences * block * channels)
        second_scale = 1.0 / math.sqrt(sequences * blocks * channels)
        first_total, second_total = call(
            functools.partial(unpack_kernel, first_scale, second_scale),
            [(blocks, blocks), (block, block)],
            0,
            me,
            mine,
            other,
            specs=[SCALAR, VMEM, VMEM],
        )
        return (
            grad_source.reshape(signal.shape),
            grad_gate.reshape(signal.shape),
            grad_kernel,
            first_total,
            second_total,
        )

    wide = P(dp, seq, None)
    return jax.shard_map(
        body,
        mesh=fine,
        in_specs=(wide, wide, wide, P(None, seq, None), P(), P()),
        out_specs=(wide, wide, P(dp, seq, None), P(), P()),
        check_vma=False,
    )
```

```python
import functools
import math

import jax
import jax.numpy as jnp
from jax import lax
from jax.experimental import pallas as pl
from jax.experimental.pallas import tpu as pltpu
from jax.sharding import Mesh, PartitionSpec as P

F32 = jnp.float32
BF16 = jnp.bfloat16
VMEM = pl.BlockSpec(memory_space=pltpu.VMEM)
PARAMS = pltpu.CompilerParams(vmem_limit_bytes=24 * 1024 * 1024)


def halves(value):
    high = value.astype(BF16)
    return high, (value - high.astype(F32)).astype(BF16)


def product(left, right, dims):
    one = lambda a, b: lax.dot_general(a, b, (dims, ((), ())), preferred_element_type=F32)
    return one(left[0], right[0]) + (one(left[0], right[1]) + one(left[1], right[0]))


NN = ((1,), (0,))
TN = ((0,), (0,))
NT = ((1,), (1,))


def enter_kernel(count, *refs):
    data, second_ref, out_ref = refs[:count], refs[count], refs[count + 2]
    held, s_ref, made = refs[count + 3:2 * count + 3], refs[2 * count + 3], refs[2 * count + 4]
    data_sem, s_sem, out_sem = refs[2 * count + 5:]
    deep, xs, near, rows, width, channels = out_ref.shape
    half = s_ref.shape[0] // near

    def fetch(row):
        return [
            pltpu.make_async_copy(data[n].at[row], held[n].at[row], data_sem.at[n, row]) for n in range(count)
        ]

    fetches = [fetch(row) for row in range(rows)]
    factors = [
        pltpu.make_async_copy(second_ref.at[pl.ds(n * half, half)], s_ref.at[pl.ds(n * half, half)], s_sem.at[n])
        for n in range(near)
    ]
    for copy in fetches[0] + factors + [copy for row in fetches[1:] for copy in row]:
        copy.start()
    seconds = []
    sends = []
    for row in range(rows):
        for copy in fetches[row]:
            copy.wait()
        value = held[0][row]
        for ref in held[1:]:
            value = value * ref[row]
        value = halves(value)
        for n in range(near):
            if row == 0:
                factors[n].wait()
                seconds.append(halves(s_ref[n * half:(n + 1) * half]))
            got = product(seconds[n], value, NN)
            made[n, :, :, row] = got.reshape(xs, deep, width, channels)
            for x in range(xs):
                copy = pltpu.make_async_copy(made.at[n, x, :, row], out_ref.at[:, x, n, row], out_sem.at[row, n, x])
                copy.start()
                sends.append(copy)
    for copy in sends:
        copy.wait()


def enter(send, flops, factor, after, *data):
    count = len(data)
    deep, xs, near, rows, width, channels = send
    size = math.prod(send) + factor.size + sum(each.size for each in data)
    return pl.pallas_call(
        functools.partial(enter_kernel, count),
        out_shape=jax.ShapeDtypeStruct(send, F32),
        in_specs=[FAR] * (count + 1) + [UNREAD],
        out_specs=FAR,
        scratch_shapes=[pltpu.VMEM(each.shape, F32) for each in data]
        + [
            pltpu.VMEM(factor.shape, F32),
            pltpu.VMEM((near, xs, deep, rows, width, channels), F32),
            pltpu.SemaphoreType.DMA((count, rows)),
            pltpu.SemaphoreType.DMA((near,)),
            pltpu.SemaphoreType.DMA((rows, near, xs)),
        ],
        compiler_params=PARAMS,
        cost_estimate=pl.CostEstimate(flops=flops, bytes_accessed=4 * size, transcendentals=0),
    )(*data, factor, after)


def lines(ref, row, nears):
    deep, xs, near, rows, width, channels = ref.shape
    return jnp.concatenate([ref[:, x, n, row].reshape(deep * width, channels) for n in nears for x in range(xs)], axis=0)


def forward_kernel(a_ref, k_ref, f_ref, z_ref, v_ref):
    first = halves(f_ref[...])
    for k in range(a_ref.shape[1]):
        z = product(first, halves(a_ref[:, k]), NN)
        z_ref[:, k] = z
        v_ref[:, k] = product(first, halves(k_ref[:, k] * z), TN)


def backward_kernel(shape, a_ref, d_ref, k_ref, z_ref, f_ref, da_ref, gk_ref, gf_ref, lines_ref):
    first = halves(f_ref[...])
    total = jnp.zeros(lines_ref.shape, F32)
    for k in range(a_ref.shape[1]):
        dv = halves(d_ref[:, k])
        dw = product(first, dv, NN)
        z = z_ref[:, k]
        weight = k_ref[:, k]
        gk_ref[:, k] = dw * z
        dz = halves(weight * dw)
        da_ref[:, k] = product(first, dz, TN)
        total += product(dv, halves(weight * z), NT) + product(halves(a_ref[:, k]), dz, NT)
    deep, xs, near, rows = shape
    for z in range(deep):
        for x in range(xs):
            for n in range(near):
                at = ((z * xs + x) * near + n) * rows
                to = ((n * xs + x) * deep + z) * rows
                lines_ref[to:to + rows] = total[at:at + rows]
    turned = lines_ref[...].T
    pieces, tall, lanes = gf_ref.shape
    low = turned.shape[0] // pieces
    gf_ref[...] = jnp.zeros(gf_ref.shape, F32)
    for piece in range(pieces):
        gf_ref[piece, :low] = turned[piece * low:(piece + 1) * low]


def leave_gates_kernel(v_ref, g_ref, c_ref, s_ref, gk_ref, gg_ref, gs_ref, same_ref):
    rows, block, channels = g_ref.shape
    second = halves(s_ref[...])
    total = jnp.zeros(gs_ref.shape, F32)
    for row in range(rows):
        v = halves(lines(v_ref, row, range(v_ref.shape[2])))
        gg_ref[row] = c_ref[row] * product(second, v, TN)
        total += product(v, halves(g_ref[row] * c_ref[row]), NT)
    gs_ref[...] = total


def half_outer(half, d_ref, x_ref, gs_ref, gf_ref, part, sem, packet):
    rows, block, channels = x_ref.shape
    pieces, tall, lanes = packet
    fetch = pltpu.make_async_copy(gs_ref.at[pl.ds(pl.multiple_of(half * (block // 2), block // 2), block // 2)], part, sem)
    fetch.start()
    total = jnp.zeros(part.shape, F32)
    for row in range(rows):
        total += product(halves(lines(d_ref, row, [half])), halves(x_ref[row]), NT)
    fetch.wait()
    total += part[...]
    high = block // (2 * pieces)
    strips = block // lanes
    return [
        (slice(strip * high, (strip + 1) * high), total[:, strip * lanes:(strip + 1) * lanes].reshape(pieces, high, lanes))
        for strip in range(strips)
    ] + [(slice(strips * high, tall), gf_ref[pl.ds(half * pieces, pieces)])]


def send_kernel(me_ref, d_ref, x_ref, gs_ref, gf_ref, after_ref, out_ref, part, sem):
    for rows, value in half_outer(1 - me_ref[0], d_ref, x_ref, gs_ref, gf_ref, part, sem, out_ref.shape):
        out_ref[:, rows] = value


def keep_kernel(me_ref, d_ref, x_ref, gs_ref, gf_ref, got_ref, out_ref, part, sem):
    for rows, value in half_outer(me_ref[0], d_ref, x_ref, gs_ref, gf_ref, part, sem, out_ref.shape):
        out_ref[:, rows] = value + got_ref[:, rows]


def sum_kernel(in_ref, after_ref, out_ref):
    total = in_ref[0]
    for part in range(1, in_ref.shape[0]):
        total += in_ref[part]
    out_ref[...] = jnp.broadcast_to(total[None], out_ref.shape)


def sum_and_pass_kernel(in_ref, after_ref, pair_ref, out_ref, same_ref):
    sum_kernel(in_ref, after_ref, out_ref)


def unpack_kernel(first_scale, second_scale, me_ref, mine_ref, other_ref, gf_ref, gs_ref):
    pieces, tall, lanes = mine_ref.shape
    block = gs_ref.shape[0]
    high = block // (2 * pieces)
    strips = block // lanes
    me = me_ref[0]
    for half, ref in ((me, mine_ref), (1 - me, other_ref)):
        rows = pl.ds(pl.multiple_of(half * (block // 2), block // 2), block // 2)
        for strip in range(strips):
            got = ref[:, strip * high:(strip + 1) * high].reshape(block // 2, lanes)
            gs_ref[rows, strip * lanes:(strip + 1) * lanes] = got * second_scale
    low = gf_ref.shape[0] // (2 * pieces)
    base = strips * high
    for piece in range(pieces):
        mine = mine_ref[piece, base:base + low] * first_scale
        other = other_ref[piece, base:base + low] * first_scale
        gf_ref[piece * low:(piece + 1) * low] = jnp.where(me == 0, mine, other)
        gf_ref[(piece + pieces) * low:(piece + pieces + 1) * low] = jnp.where(me == 0, other, mine)


def leave_signal_kernel(d_ref, s_ref, gx_ref, token_ref):
    token_ref[...] = jnp.zeros(token_ref.shape, F32)
    rows, block, channels = gx_ref.shape
    second = halves(s_ref[...])
    for row in range(rows):
        gx_ref[row] = product(second, halves(lines(d_ref, row, range(d_ref.shape[2]))), TN)


SCALAR = pl.BlockSpec(memory_space=pltpu.SMEM)
UNREAD = pl.BlockSpec(memory_space=pl.ANY)
FAR = pl.BlockSpec(memory_space=pltpu.HBM)


def call(kernel, outs, flops, *args, specs=None, out_specs=None, aliases=None, scratch=()):
    size = sum(math.prod(shape) for shape in outs) + sum(arg.size for arg in args)
    return pl.pallas_call(
        kernel,
        out_shape=[jax.ShapeDtypeStruct(shape, F32) for shape in outs],
        in_specs=specs or [VMEM] * len(args),
        out_specs=out_specs or [VMEM] * len(outs),
        input_output_aliases=aliases or {},
        scratch_shapes=list(scratch),
        compiler_params=PARAMS,
        cost_estimate=pl.CostEstimate(flops=flops, bytes_accessed=4 * size, transcendentals=0),
    )(*args)


def exchange(data, axes):
    return lax.all_to_all(data, axes, split_axis=0, concat_axis=0, tiled=True)


def swap(data, axis):
    return lax.ppermute(data, axis, [(0, 1), (1, 0)])


def pick(data, axis, index):
    return lax.dynamic_index_in_dim(data, index, axis, keepdims=False)


def halve_sum(data, axis, name):
    me = lax.axis_index(name)
    return pick(data, axis, me) + swap(pick(data, axis, 1 - me), name)


def solution(mesh):
    seq = ("near", "x", "z")
    order = ("z", "x", "near")
    dp = ("far", "core")
    shape = dict(mesh.shape)
    near = 2
    xs = 4
    fine = Mesh(
        mesh.devices.reshape(near, xs, shape["seq"] // (near * xs), shape["dp"] // 2, 2),
        seq + dp,
    )

    def body(signal, gate_values, cotangent, kernel, first_factor, second_factor):
        blocks = first_factor.shape[0]
        block = second_factor.shape[0]
        channels = signal.shape[2]
        peers = lax.axis_size(seq)
        rows = signal.shape[1] // block
        width = block // peers
        near, xs, deep = (lax.axis_size(name) for name in seq)
        send = (deep, xs, near, rows, width, channels)
        flat = (peers, rows, width, channels)
        side = (blocks, width, channels)
        place = (rows, block, channels)
        source = signal.reshape(place)
        gating = gate_values.reshape(place)
        upstream = cotangent.reshape(place)
        second_flops = 6 * rows * block * block * channels
        first_flops = 6 * blocks * blocks * width * channels
        turned = first_factor.reshape(blocks, near, xs, deep, rows).transpose(0, 3, 2, 1, 4).reshape(blocks, blocks)
        turn = first_factor[:8]
        for _ in range(4):
            turn = lax.ppermute(turn, ("x", "core"), [(2 * x + 1, (2 * x + 3) % (2 * xs)) for x in range(xs)])
        section = enter(send, second_flops, second_factor, turn, source)
        lanes = 128
        across = ("near", "x", "far")
        pieces = lax.axis_size(across)
        low = -(-blocks // (16 * pieces)) * 8
        tall = block * block // (2 * lanes * pieces) + low
        section = exchange(section.reshape(flat), order).reshape(side)
        grad_back = enter(send, second_flops, second_factor, turn, gating, upstream)
        grad_back = exchange(grad_back.reshape(flat), order).reshape(side)
        spectrum, back = call(forward_kernel, [side, side], 2 * first_flops, section, kernel, turned)
        back = exchange(back.reshape(flat), order).reshape(send)
        grad_section, grad_kernel, grad_first = call(
            functools.partial(backward_kernel, (deep, xs, near, rows)),
            [side, side, (2 * pieces, low, lanes)],
            4 * first_flops,
            section,
            grad_back,
            kernel,
            spectrum,
            turned,
            scratch=[pltpu.VMEM((blocks, blocks), F32)],
        )
        grad_section = exchange(grad_section.reshape(flat), order).reshape(send)
        grad_gate, second_part, grad_kernel = call(
            leave_gates_kernel,
            [place, (block, block), side],
            2 * second_flops,
            back,
            gating,
            upstream,
            second_factor,
            grad_kernel,
            specs=[VMEM] * 4 + [UNREAD],
            out_specs=[VMEM] * 2 + [UNREAD],
            aliases={4: 2},
        )
        sequences = lax.axis_size(dp)
        grad_kernel = grad_kernel.reshape(sequences // 2, 2, blocks // sequences, width, channels)
        kernel_pair = halve_sum(grad_kernel, 1, "core")
        me = lax.axis_index("core").reshape(1)
        packet = (pieces, tall, lanes)
        outer_args = (me, grad_section, source, second_part, grad_first)
        outer_specs = [SCALAR, VMEM, VMEM, FAR, VMEM]
        scratch = [pltpu.VMEM((block // 2, block), F32), pltpu.SemaphoreType.DMA]
        (half,) = call(
            send_kernel,
            [packet],
            second_flops // 2,
            *outer_args,
            kernel_pair[0, :1],
            specs=outer_specs + [UNREAD],
            scratch=scratch,
        )
        half = swap(half, "core")
        (half,) = call(
            keep_kernel, [packet], second_flops // 2, *outer_args, half, specs=outer_specs + [VMEM], scratch=scratch
        )
        grad_source, token = call(leave_signal_kernel, [place, (8, lanes)], second_flops, grad_section, second_factor)
        part, kernel_pair = call(
            sum_and_pass_kernel,
            [(deep, tall, lanes), kernel_pair.shape],
            0,
            exchange(half, across),
            token,
            kernel_pair,
            specs=[VMEM, UNREAD, UNREAD],
            out_specs=[VMEM, UNREAD],
            aliases={2: 1},
        )
        grad_kernel = halve_sum(kernel_pair, 0, "far")
        part = exchange(part, "z")
        (part,) = call(sum_kernel, [packet], 0, part, grad_kernel[:1], specs=[VMEM, UNREAD])
        mine = exchange(part, across)
        other = swap(mine, "core")
        first_scale = 1.0 / math.sqrt(sequences * block * channels)
        second_scale = 1.0 / math.sqrt(sequences * blocks * channels)
        first_total, second_total = call(
            functools.partial(unpack_kernel, first_scale, second_scale),
            [(blocks, blocks), (block, block)],
            0,
            me,
            mine,
            other,
            specs=[SCALAR, VMEM, VMEM],
        )
        return (
            grad_source.reshape(signal.shape),
            grad_gate.reshape(signal.shape),
            grad_kernel,
            first_total,
            second_total,
        )

    wide = P(dp, seq, None)
    return jax.shard_map(
        body,
        mesh=fine,
        in_specs=(wide, wide, wide, P(None, seq, None), P(), P()),
        out_specs=(wide, wide, P(dp, seq, None), P(), P()),
        check_vma=False,
    )
```

```python
import functools
import math

import jax
import jax.numpy as jnp
from jax import lax
from jax.experimental import pallas as pl
from jax.experimental.pallas import tpu as pltpu
from jax.sharding import Mesh, PartitionSpec as P

F32 = jnp.float32
BF16 = jnp.bfloat16
VMEM = pl.BlockSpec(memory_space=pltpu.VMEM)
PARAMS = pltpu.CompilerParams(vmem_limit_bytes=24 * 1024 * 1024)
WIDE = pltpu.CompilerParams(vmem_limit_bytes=62 * 1024 * 1024)


def halves(value):
    high = value.astype(BF16)
    return high, (value - high.astype(F32)).astype(BF16)


def product(left, right, dims):
    one = lambda a, b: lax.dot_general(a, b, (dims, ((), ())), preferred_element_type=F32)
    return one(left[0], right[0]) + (one(left[0], right[1]) + one(left[1], right[0]))


NN = ((1,), (0,))
TN = ((0,), (0,))
NT = ((1,), (1,))


def enter_kernel(count, *refs):
    data, second_ref, out_ref = refs[:count], refs[count], refs[count + 2]
    held, s_ref, made = refs[count + 3:2 * count + 3], refs[2 * count + 3], refs[2 * count + 4]
    data_sem, s_sem, out_sem = refs[2 * count + 5:]
    deep, xs, near, rows, width, channels = out_ref.shape
    half = s_ref.shape[0] // near

    def fetch(row):
        return [
            pltpu.make_async_copy(data[n].at[row], held[n].at[row], data_sem.at[n, row]) for n in range(count)
        ]

    fetches = [fetch(row) for row in range(rows)]
    factors = [
        pltpu.make_async_copy(second_ref.at[pl.ds(n * half, half)], s_ref.at[pl.ds(n * half, half)], s_sem.at[n])
        for n in range(near)
    ]
    for copy in fetches[0] + factors + [copy for row in fetches[1:] for copy in row]:
        copy.start()
    seconds = []
    sends = []
    for row in range(rows):
        for copy in fetches[row]:
            copy.wait()
        value = held[0][row]
        for ref in held[1:]:
            value = value * ref[row]
        value = halves(value)
        for n in range(near):
            if row == 0:
                factors[n].wait()
                seconds.append(halves(s_ref[n * half:(n + 1) * half]))
            got = product(seconds[n], value, NN)
            made[n, :, :, row] = got.reshape(xs, deep, width, channels)
            for x in range(xs):
                copy = pltpu.make_async_copy(made.at[n, x, :, row], out_ref.at[:, x, n, row], out_sem.at[row, n, x])
                copy.start()
                sends.append(copy)
    for copy in sends:
        copy.wait()


def enter(send, flops, factor, after, *data):
    count = len(data)
    deep, xs, near, rows, width, channels = send
    size = math.prod(send) + factor.size + sum(each.size for each in data)
    return pl.pallas_call(
        functools.partial(enter_kernel, count),
        out_shape=jax.ShapeDtypeStruct(send, F32),
        in_specs=[FAR] * (count + 1) + [UNREAD],
        out_specs=FAR,
        scratch_shapes=[pltpu.VMEM(each.shape, F32) for each in data]
        + [
            pltpu.VMEM(factor.shape, F32),
            pltpu.VMEM((near, xs, deep, rows, width, channels), F32),
            pltpu.SemaphoreType.DMA((count, rows)),
            pltpu.SemaphoreType.DMA((near,)),
            pltpu.SemaphoreType.DMA((rows, near, xs)),
        ],
        compiler_params=WIDE,
        cost_estimate=pl.CostEstimate(flops=flops, bytes_accessed=4 * size, transcendentals=0),
    )(*data, factor, after)


def lines(ref, row, nears):
    deep, xs, near, rows, width, channels = ref.shape
    return jnp.concatenate([ref[:, x, n, row].reshape(deep * width, channels) for n in nears for x in range(xs)], axis=0)


def forward_kernel(a_ref, k_ref, f_ref, z_ref, v_ref):
    first = halves(f_ref[...])
    for k in range(a_ref.shape[1]):
        z = product(first, halves(a_ref[:, k]), NN)
        z_ref[:, k] = z
        v_ref[:, k] = product(first, halves(k_ref[:, k] * z), TN)


def backward_kernel(shape, a_ref, d_ref, k_ref, z_ref, f_ref, da_ref, gk_ref, gf_ref, lines_ref):
    first = halves(f_ref[...])
    total = jnp.zeros(lines_ref.shape, F32)
    for k in range(a_ref.shape[1]):
        dv = halves(d_ref[:, k])
        dw = product(first, dv, NN)
        z = z_ref[:, k]
        weight = k_ref[:, k]
        gk_ref[:, k] = dw * z
        dz = halves(weight * dw)
        da_ref[:, k] = product(first, dz, TN)
        total += product(dv, halves(weight * z), NT) + product(halves(a_ref[:, k]), dz, NT)
    deep, xs, near, rows = shape
    for z in range(deep):
        for x in range(xs):
            for n in range(near):
                at = ((z * xs + x) * near + n) * rows
                to = ((n * xs + x) * deep + z) * rows
                lines_ref[to:to + rows] = total[at:at + rows]
    turned = lines_ref[...].T
    pieces, tall, lanes = gf_ref.shape
    low = turned.shape[0] // pieces
    gf_ref[...] = jnp.zeros(gf_ref.shape, F32)
    for piece in range(pieces):
        gf_ref[piece, :low] = turned[piece * low:(piece + 1) * low]


def leave_gates_kernel(v_ref, g_ref, c_ref, s_ref, gk_ref, gg_ref, gs_ref, same_ref):
    rows, block, channels = g_ref.shape
    second = halves(s_ref[...])
    total = jnp.zeros(gs_ref.shape, F32)
    for row in range(rows):
        v = halves(lines(v_ref, row, range(v_ref.shape[2])))
        gg_ref[row] = c_ref[row] * product(second, v, TN)
        total += product(v, halves(g_ref[row] * c_ref[row]), NT)
    gs_ref[...] = total


def half_outer(half, d_ref, x_ref, gs_ref, gf_ref, part, sem, packet):
    rows, block, channels = x_ref.shape
    pieces, tall, lanes = packet
    fetch = pltpu.make_async_copy(gs_ref.at[pl.ds(pl.multiple_of(half * (block // 2), block // 2), block // 2)], part, sem)
    fetch.start()
    total = jnp.zeros(part.shape, F32)
    for row in range(rows):
        total += product(halves(lines(d_ref, row, [half])), halves(x_ref[row]), NT)
    fetch.wait()
    total += part[...]
    high = block // (2 * pieces)
    strips = block // lanes
    return [
        (slice(strip * high, (strip + 1) * high), total[:, strip * lanes:(strip + 1) * lanes].reshape(pieces, high, lanes))
        for strip in range(strips)
    ] + [(slice(strips * high, tall), gf_ref[pl.ds(half * pieces, pieces)])]


def send_kernel(me_ref, d_ref, x_ref, gs_ref, gf_ref, after_ref, out_ref, part, sem):
    for rows, value in half_outer(1 - me_ref[0], d_ref, x_ref, gs_ref, gf_ref, part, sem, out_ref.shape):
        out_ref[:, rows] = value


def keep_kernel(me_ref, d_ref, x_ref, gs_ref, gf_ref, got_ref, out_ref, part, sem):
    for rows, value in half_outer(me_ref[0], d_ref, x_ref, gs_ref, gf_ref, part, sem, out_ref.shape):
        out_ref[:, rows] = value + got_ref[:, rows]


def sum_kernel(in_ref, after_ref, out_ref):
    total = in_ref[0]
    for part in range(1, in_ref.shape[0]):
        total += in_ref[part]
    out_ref[...] = jnp.broadcast_to(total[None], out_ref.shape)


def unpack_kernel(first_scale, second_scale, me_ref, mine_ref, other_ref, gf_ref, gs_ref):
    pieces, tall, lanes = mine_ref.shape
    block = gs_ref.shape[0]
    high = block // (2 * pieces)
    strips = block // lanes
    me = me_ref[0]
    for half, ref in ((me, mine_ref), (1 - me, other_ref)):
        rows = pl.ds(pl.multiple_of(half * (block // 2), block // 2), block // 2)
        for strip in range(strips):
            got = ref[:, strip * high:(strip + 1) * high].reshape(block // 2, lanes)
            gs_ref[rows, strip * lanes:(strip + 1) * lanes] = got * second_scale
    low = gf_ref.shape[0] // (2 * pieces)
    base = strips * high
    for piece in range(pieces):
        mine = mine_ref[piece, base:base + low] * first_scale
        other = other_ref[piece, base:base + low] * first_scale
        gf_ref[piece * low:(piece + 1) * low] = jnp.where(me == 0, mine, other)
        gf_ref[(piece + pieces) * low:(piece + pieces + 1) * low] = jnp.where(me == 0, other, mine)


def leave_signal_kernel(d_ref, s_ref, gx_ref, token_ref):
    token_ref[...] = jnp.zeros(token_ref.shape, F32)
    rows, block, channels = gx_ref.shape
    second = halves(s_ref[...])
    for row in range(rows):
        gx_ref[row] = product(second, halves(lines(d_ref, row, range(d_ref.shape[2]))), TN)


SCALAR = pl.BlockSpec(memory_space=pltpu.SMEM)
UNREAD = pl.BlockSpec(memory_space=pl.ANY)
FAR = pl.BlockSpec(memory_space=pltpu.HBM)


def call(kernel, outs, flops, *args, specs=None, out_specs=None, aliases=None, scratch=()):
    size = sum(math.prod(shape) for shape in outs) + sum(arg.size for arg in args)
    return pl.pallas_call(
        kernel,
        out_shape=[jax.ShapeDtypeStruct(shape, F32) for shape in outs],
        in_specs=specs or [VMEM] * len(args),
        out_specs=out_specs or [VMEM] * len(outs),
        input_output_aliases=aliases or {},
        scratch_shapes=list(scratch),
        compiler_params=PARAMS,
        cost_estimate=pl.CostEstimate(flops=flops, bytes_accessed=4 * size, transcendentals=0),
    )(*args)


def exchange(data, axes):
    return lax.all_to_all(data, axes, split_axis=0, concat_axis=0, tiled=True)


def swap(data, axis):
    return lax.ppermute(data, axis, [(0, 1), (1, 0)])


def pick(data, axis, index):
    return lax.dynamic_index_in_dim(data, index, axis, keepdims=False)


def halve_sum(data, axis, name):
    me = lax.axis_index(name)
    return pick(data, axis, me) + swap(pick(data, axis, 1 - me), name)


def solution(mesh):
    seq = ("near", "x", "z")
    order = ("z", "x", "near")
    dp = ("far", "core")
    shape = dict(mesh.shape)
    near = 2
    xs = 4
    fine = Mesh(
        mesh.devices.reshape(near, xs, shape["seq"] // (near * xs), shape["dp"] // 2, 2),
        seq + dp,
    )

    def body(signal, gate_values, cotangent, kernel, first_factor, second_factor):
        blocks = first_factor.shape[0]
        block = second_factor.shape[0]
        channels = signal.shape[2]
        peers = lax.axis_size(seq)
        rows = signal.shape[1] // block
        width = block // peers
        near, xs, deep = (lax.axis_size(name) for name in seq)
        send = (deep, xs, near, rows, width, channels)
        flat = (peers, rows, width, channels)
        side = (blocks, width, channels)
        place = (rows, block, channels)
        source = signal.reshape(place)
        gating = gate_values.reshape(place)
        upstream = cotangent.reshape(place)
        second_flops = 6 * rows * block * block * channels
        first_flops = 6 * blocks * blocks * width * channels
        turned = first_factor.reshape(blocks, near, xs, deep, rows).transpose(0, 3, 2, 1, 4).reshape(blocks, blocks)
        turn = first_factor[:8]
        for _ in range(4):
            turn = lax.ppermute(turn, ("x", "core"), [(2 * x + 1, (2 * x + 3) % (2 * xs)) for x in range(xs)])
        section = enter(send, second_flops, second_factor, turn, source)
        lanes = 128
        across = ("near", "x", "far")
        pieces = lax.axis_size(across)
        low = -(-blocks // (16 * pieces)) * 8
        tall = block * block // (2 * lanes * pieces) + low
        section = exchange(section.reshape(flat), order).reshape(side)
        grad_back = enter(send, second_flops, second_factor, turn, gating, upstream)
        grad_back = exchange(grad_back.reshape(flat), order).reshape(side)
        spectrum, back = call(forward_kernel, [side, side], 2 * first_flops, section, kernel, turned)
        back = exchange(back.reshape(flat), order).reshape(send)
        grad_section, grad_kernel, grad_first = call(
            functools.partial(backward_kernel, (deep, xs, near, rows)),
            [side, side, (2 * pieces, low, lanes)],
            4 * first_flops,
            section,
            grad_back,
            kernel,
            spectrum,
            turned,
            scratch=[pltpu.VMEM((blocks, blocks), F32)],
        )
        grad_section = exchange(grad_section.reshape(flat), order).reshape(send)
        grad_gate, second_part, grad_kernel = call(
            leave_gates_kernel,
            [place, (block, block), side],
            2 * second_flops,
            back,
            gating,
            upstream,
            second_factor,
            grad_kernel,
            specs=[VMEM] * 4 + [UNREAD],
            out_specs=[VMEM] * 2 + [UNREAD],
            aliases={4: 2},
        )
        sequences = lax.axis_size(dp)
        grad_kernel = grad_kernel.reshape(sequences // 2, 2, blocks // sequences, width, channels)
        kernel_pair = halve_sum(grad_kernel, 1, "core")
        grad_kernel = halve_sum(kernel_pair, 0, "far")
        me = lax.axis_index("core").reshape(1)
        packet = (pieces, tall, lanes)
        outer_args = (me, grad_section, source, second_part, grad_first)
        outer_specs = [SCALAR, VMEM, VMEM, FAR, VMEM]
        scratch = [pltpu.VMEM((block // 2, block), F32), pltpu.SemaphoreType.DMA]
        (half,) = call(
            send_kernel,
            [packet],
            second_flops // 2,
            *outer_args,
            kernel_pair[0, :1],
            specs=outer_specs + [UNREAD],
            scratch=scratch,
        )
        half = swap(half, "core")
        (half,) = call(
            keep_kernel, [packet], second_flops // 2, *outer_args, half, specs=outer_specs + [VMEM], scratch=scratch
        )
        grad_source, token = call(leave_signal_kernel, [place, (8, lanes)], second_flops, grad_section, second_factor)
        (part,) = call(sum_kernel, [(deep, tall, lanes)], 0, exchange(half, across), token, specs=[VMEM, UNREAD])
        part = exchange(part, "z")
        (part,) = call(sum_kernel, [packet], 0, part, grad_kernel[:1], specs=[VMEM, UNREAD])
        mine = exchange(part, across)
        other = swap(mine, "core")
        first_scale = 1.0 / math.sqrt(sequences * block * channels)
        second_scale = 1.0 / math.sqrt(sequences * blocks * channels)
        first_total, second_total = call(
            functools.partial(unpack_kernel, first_scale, second_scale),
            [(blocks, blocks), (block, block)],
            0,
            me,
            mine,
            other,
            specs=[SCALAR, VMEM, VMEM],
        )
        return (
            grad_source.reshape(signal.shape),
            grad_gate.reshape(signal.shape),
            grad_kernel,
            first_total,
            second_total,
        )

    wide = P(dp, seq, None)
    return jax.shard_map(
        body,
        mesh=fine,
        in_specs=(wide, wide, wide, P(None, seq, None), P(), P()),
        out_specs=(wide, wide, P(dp, seq, None), P(), P()),
        check_vma=False,
    )
```

```python
import functools
import math

import jax
import jax.numpy as jnp
from jax import lax
from jax.experimental import pallas as pl
from jax.experimental.pallas import tpu as pltpu
from jax.sharding import Mesh, PartitionSpec as P

F32 = jnp.float32
BF16 = jnp.bfloat16
VMEM = pl.BlockSpec(memory_space=pltpu.VMEM)
PARAMS = pltpu.CompilerParams(vmem_limit_bytes=24 * 1024 * 1024)
WIDE = pltpu.CompilerParams(vmem_limit_bytes=62 * 1024 * 1024)


def halves(value):
    high = value.astype(BF16)
    return high, (value - high.astype(F32)).astype(BF16)


def product(left, right, dims):
    one = lambda a, b: lax.dot_general(a, b, (dims, ((), ())), preferred_element_type=F32)
    return one(left[0], right[0]) + (one(left[0], right[1]) + one(left[1], right[0]))


NN = ((1,), (0,))
TN = ((0,), (0,))
NT = ((1,), (1,))


def enter_kernel(count, *refs):
    data, second_ref, out_ref = refs[:count], refs[count], refs[count + 2]
    held, s_ref, made = refs[count + 3:2 * count + 3], refs[2 * count + 3], refs[2 * count + 4]
    data_sem, s_sem, out_sem = refs[2 * count + 5:]
    deep, xs, near, rows, width, channels = out_ref.shape
    half = s_ref.shape[0] // near

    def fetch(row):
        return [
            pltpu.make_async_copy(data[n].at[row], held[n].at[row], data_sem.at[n, row]) for n in range(count)
        ]

    fetches = [fetch(row) for row in range(rows)]
    factors = [
        pltpu.make_async_copy(second_ref.at[pl.ds(n * half, half)], s_ref.at[pl.ds(n * half, half)], s_sem.at[n])
        for n in range(near)
    ]
    for copy in fetches[0] + factors + [copy for row in fetches[1:] for copy in row]:
        copy.start()
    seconds = []
    sends = []
    for row in range(rows):
        for copy in fetches[row]:
            copy.wait()
        value = held[0][row]
        for ref in held[1:]:
            value = value * ref[row]
        value = halves(value)
        for n in range(near):
            if row == 0:
                factors[n].wait()
                seconds.append(halves(s_ref[n * half:(n + 1) * half]))
            got = product(seconds[n], value, NN)
            made[n, :, :, row] = got.reshape(xs, deep, width, channels)
            for x in range(xs):
                copy = pltpu.make_async_copy(made.at[n, x, :, row], out_ref.at[:, x, n, row], out_sem.at[row, n, x])
                copy.start()
                sends.append(copy)
    for copy in sends:
        copy.wait()


def enter(send, flops, factor, after, *data):
    count = len(data)
    deep, xs, near, rows, width, channels = send
    size = math.prod(send) + factor.size + sum(each.size for each in data)
    return pl.pallas_call(
        functools.partial(enter_kernel, count),
        out_shape=jax.ShapeDtypeStruct(send, F32),
        in_specs=[FAR] * (count + 1) + [UNREAD],
        out_specs=FAR,
        scratch_shapes=[pltpu.VMEM(each.shape, F32) for each in data]
        + [
            pltpu.VMEM(factor.shape, F32),
            pltpu.VMEM((near, xs, deep, rows, width, channels), F32),
            pltpu.SemaphoreType.DMA((count, rows)),
            pltpu.SemaphoreType.DMA((near,)),
            pltpu.SemaphoreType.DMA((rows, near, xs)),
        ],
        compiler_params=WIDE,
        cost_estimate=pl.CostEstimate(flops=flops, bytes_accessed=4 * size, transcendentals=0),
    )(*data, factor, after)


def lines(ref, row, nears):
    deep, xs, near, rows, width, channels = ref.shape
    return jnp.concatenate([ref[:, x, n, row].reshape(deep * width, channels) for n in nears for x in range(xs)], axis=0)


def forward_kernel(a_ref, k_ref, f_ref, v_ref):
    first = halves(f_ref[...])
    for k in range(a_ref.shape[1]):
        z = product(first, halves(a_ref[:, k]), NN)
        v_ref[:, k] = product(first, halves(k_ref[:, k] * z), TN)


def backward_kernel(shape, a_ref, d_ref, k_ref, f_ref, da_ref, gk_ref, gf_ref, lines_ref):
    first = halves(f_ref[...])
    total = jnp.zeros(lines_ref.shape, F32)
    for k in range(a_ref.shape[1]):
        dv = halves(d_ref[:, k])
        dw = product(first, dv, NN)
        section = halves(a_ref[:, k])
        z = product(first, section, NN)
        weight = k_ref[:, k]
        gk_ref[:, k] = dw * z
        dz = halves(weight * dw)
        da_ref[:, k] = product(first, dz, TN)
        total += product(dv, halves(weight * z), NT) + product(section, dz, NT)
    deep, xs, near, rows = shape
    for z in range(deep):
        for x in range(xs):
            for n in range(near):
                at = ((z * xs + x) * near + n) * rows
                to = ((n * xs + x) * deep + z) * rows
                lines_ref[to:to + rows] = total[at:at + rows]
    turned = lines_ref[...].T
    pieces, tall, lanes = gf_ref.shape
    low = turned.shape[0] // pieces
    gf_ref[...] = jnp.zeros(gf_ref.shape, F32)
    for piece in range(pieces):
        gf_ref[piece, :low] = turned[piece * low:(piece + 1) * low]


def leave_gates_kernel(v_ref, g_ref, c_ref, s_ref, gk_ref, gg_ref, gs_ref, same_ref):
    rows, block, channels = g_ref.shape
    second = halves(s_ref[...])
    total = jnp.zeros(gs_ref.shape, F32)
    for row in range(rows):
        v = halves(lines(v_ref, row, range(v_ref.shape[2])))
        gg_ref[row] = c_ref[row] * product(second, v, TN)
        total += product(v, halves(g_ref[row] * c_ref[row]), NT)
    gs_ref[...] = total


def half_outer(half, d_ref, x_ref, gs_ref, gf_ref, part, sem, packet):
    rows, block, channels = x_ref.shape
    pieces, tall, lanes = packet
    fetch = pltpu.make_async_copy(gs_ref.at[pl.ds(pl.multiple_of(half * (block // 2), block // 2), block // 2)], part, sem)
    fetch.start()
    total = jnp.zeros(part.shape, F32)
    for row in range(rows):
        total += product(halves(lines(d_ref, row, [half])), halves(x_ref[row]), NT)
    fetch.wait()
    total += part[...]
    high = block // (2 * pieces)
    strips = block // lanes
    return [
        (slice(strip * high, (strip + 1) * high), total[:, strip * lanes:(strip + 1) * lanes].reshape(pieces, high, lanes))
        for strip in range(strips)
    ] + [(slice(strips * high, tall), gf_ref[pl.ds(half * pieces, pieces)])]


def send_kernel(me_ref, d_ref, x_ref, gs_ref, gf_ref, after_ref, out_ref, part, sem):
    for rows, value in half_outer(1 - me_ref[0], d_ref, x_ref, gs_ref, gf_ref, part, sem, out_ref.shape):
        out_ref[:, rows] = value


def keep_kernel(me_ref, d_ref, x_ref, gs_ref, gf_ref, got_ref, out_ref, part, sem):
    for rows, value in half_outer(me_ref[0], d_ref, x_ref, gs_ref, gf_ref, part, sem, out_ref.shape):
        out_ref[:, rows] = value + got_ref[:, rows]


def sum_kernel(in_ref, after_ref, out_ref):
    total = in_ref[0]
    for part in range(1, in_ref.shape[0]):
        total += in_ref[part]
    out_ref[...] = jnp.broadcast_to(total[None], out_ref.shape)


def unpack_kernel(first_scale, second_scale, me_ref, mine_ref, other_ref, gf_ref, gs_ref):
    pieces, tall, lanes = mine_ref.shape
    block = gs_ref.shape[0]
    high = block // (2 * pieces)
    strips = block // lanes
    me = me_ref[0]
    for half, ref in ((me, mine_ref), (1 - me, other_ref)):
        rows = pl.ds(pl.multiple_of(half * (block // 2), block // 2), block // 2)
        for strip in range(strips):
            got = ref[:, strip * high:(strip + 1) * high].reshape(block // 2, lanes)
            gs_ref[rows, strip * lanes:(strip + 1) * lanes] = got * second_scale
    low = gf_ref.shape[0] // (2 * pieces)
    base = strips * high
    for piece in range(pieces):
        mine = mine_ref[piece, base:base + low] * first_scale
        other = other_ref[piece, base:base + low] * first_scale
        gf_ref[piece * low:(piece + 1) * low] = jnp.where(me == 0, mine, other)
        gf_ref[(piece + pieces) * low:(piece + pieces + 1) * low] = jnp.where(me == 0, other, mine)


def leave_signal_kernel(d_ref, s_ref, gx_ref, token_ref):
    token_ref[...] = jnp.zeros(token_ref.shape, F32)
    rows, block, channels = gx_ref.shape
    second = halves(s_ref[...])
    for row in range(rows):
        gx_ref[row] = product(second, halves(lines(d_ref, row, range(d_ref.shape[2]))), TN)


SCALAR = pl.BlockSpec(memory_space=pltpu.SMEM)
UNREAD = pl.BlockSpec(memory_space=pl.ANY)
FAR = pl.BlockSpec(memory_space=pltpu.HBM)


def call(kernel, outs, flops, *args, specs=None, out_specs=None, aliases=None, scratch=()):
    size = sum(math.prod(shape) for shape in outs) + sum(arg.size for arg in args)
    return pl.pallas_call(
        kernel,
        out_shape=[jax.ShapeDtypeStruct(shape, F32) for shape in outs],
        in_specs=specs or [VMEM] * len(args),
        out_specs=out_specs or [VMEM] * len(outs),
        input_output_aliases=aliases or {},
        scratch_shapes=list(scratch),
        compiler_params=PARAMS,
        cost_estimate=pl.CostEstimate(flops=flops, bytes_accessed=4 * size, transcendentals=0),
    )(*args)


def exchange(data, axes):
    return lax.all_to_all(data, axes, split_axis=0, concat_axis=0, tiled=True)


def swap(data, axis):
    return lax.ppermute(data, axis, [(0, 1), (1, 0)])


def pick(data, axis, index):
    return lax.dynamic_index_in_dim(data, index, axis, keepdims=False)


def halve_sum(data, axis, name):
    me = lax.axis_index(name)
    return pick(data, axis, me) + swap(pick(data, axis, 1 - me), name)


def solution(mesh):
    seq = ("near", "x", "z")
    order = ("z", "x", "near")
    dp = ("far", "core")
    shape = dict(mesh.shape)
    near = 2
    xs = 4
    fine = Mesh(
        mesh.devices.reshape(near, xs, shape["seq"] // (near * xs), shape["dp"] // 2, 2),
        seq + dp,
    )

    def body(signal, gate_values, cotangent, kernel, first_factor, second_factor):
        blocks = first_factor.shape[0]
        block = second_factor.shape[0]
        channels = signal.shape[2]
        peers = lax.axis_size(seq)
        rows = signal.shape[1] // block
        width = block // peers
        near, xs, deep = (lax.axis_size(name) for name in seq)
        send = (deep, xs, near, rows, width, channels)
        flat = (peers, rows, width, channels)
        side = (blocks, width, channels)
        place = (rows, block, channels)
        source = signal.reshape(place)
        gating = gate_values.reshape(place)
        upstream = cotangent.reshape(place)
        second_flops = 6 * rows * block * block * channels
        first_flops = 6 * blocks * blocks * width * channels
        turned = first_factor.reshape(blocks, near, xs, deep, rows).transpose(0, 3, 2, 1, 4).reshape(blocks, blocks)
        turn = first_factor[:8]
        for _ in range(4):
            turn = lax.ppermute(turn, ("x", "core"), [(2 * x + 1, (2 * x + 3) % (2 * xs)) for x in range(xs)])
        section = enter(send, second_flops, second_factor, turn, source)
        lanes = 128
        across = ("near", "x", "far")
        pieces = lax.axis_size(across)
        low = -(-blocks // (16 * pieces)) * 8
        tall = block * block // (2 * lanes * pieces) + low
        section = exchange(section.reshape(flat), order).reshape(side)
        grad_back = enter(send, second_flops, second_factor, turn, gating, upstream)
        grad_back = exchange(grad_back.reshape(flat), order).reshape(side)
        (back,) = call(forward_kernel, [side], 2 * first_flops, section, kernel, turned)
        back = exchange(back.reshape(flat), order).reshape(send)
        grad_section, grad_kernel, grad_first = call(
            functools.partial(backward_kernel, (deep, xs, near, rows)),
            [side, side, (2 * pieces, low, lanes)],
            5 * first_flops,
            section,
            grad_back,
            kernel,
            turned,
            scratch=[pltpu.VMEM((blocks, blocks), F32)],
        )
        grad_section = exchange(grad_section.reshape(flat), order).reshape(send)
        grad_gate, second_part, grad_kernel = call(
            leave_gates_kernel,
            [place, (block, block), side],
            2 * second_flops,
            back,
            gating,
            upstream,
            second_factor,
            grad_kernel,
            specs=[VMEM] * 4 + [UNREAD],
            out_specs=[VMEM] * 2 + [UNREAD],
            aliases={4: 2},
        )
        sequences = lax.axis_size(dp)
        grad_kernel = grad_kernel.reshape(sequences // 2, 2, blocks // sequences, width, channels)
        kernel_pair = halve_sum(grad_kernel, 1, "core")
        grad_kernel = halve_sum(kernel_pair, 0, "far")
        me = lax.axis_index("core").reshape(1)
        packet = (pieces, tall, lanes)
        outer_args = (me, grad_section, source, second_part, grad_first)
        outer_specs = [SCALAR, VMEM, VMEM, FAR, VMEM]
        scratch = [pltpu.VMEM((block // 2, block), F32), pltpu.SemaphoreType.DMA]
        (half,) = call(
            send_kernel,
            [packet],
            second_flops // 2,
            *outer_args,
            kernel_pair[0, :1],
            specs=outer_specs + [UNREAD],
            scratch=scratch,
        )
        half = swap(half, "core")
        (half,) = call(
            keep_kernel, [packet], second_flops // 2, *outer_args, half, specs=outer_specs + [VMEM], scratch=scratch
        )
        grad_source, token = call(leave_signal_kernel, [place, (8, lanes)], second_flops, grad_section, second_factor)
        (part,) = call(sum_kernel, [(deep, tall, lanes)], 0, exchange(half, across), token, specs=[VMEM, UNREAD])
        part = exchange(part, "z")
        (part,) = call(sum_kernel, [packet], 0, part, grad_kernel[:1], specs=[VMEM, UNREAD])
        mine = exchange(part, across)
        other = swap(mine, "core")
        first_scale = 1.0 / math.sqrt(sequences * block * channels)
        second_scale = 1.0 / math.sqrt(sequences * blocks * channels)
        first_total, second_total = call(
            functools.partial(unpack_kernel, first_scale, second_scale),
            [(blocks, blocks), (block, block)],
            0,
            me,
            mine,
            other,
            specs=[SCALAR, VMEM, VMEM],
        )
        return (
            grad_source.reshape(signal.shape),
            grad_gate.reshape(signal.shape),
            grad_kernel,
            first_total,
            second_total,
        )

    wide = P(dp, seq, None)
    return jax.shard_map(
        body,
        mesh=fine,
        in_specs=(wide, wide, wide, P(None, seq, None), P(), P()),
        out_specs=(wide, wide, P(dp, seq, None), P(), P()),
        check_vma=False,
    )
```

```python
import functools
import math

import jax
import jax.numpy as jnp
from jax import lax
from jax.experimental import pallas as pl
from jax.experimental.pallas import tpu as pltpu
from jax.sharding import Mesh, PartitionSpec as P

F32 = jnp.float32
BF16 = jnp.bfloat16
VMEM = pl.BlockSpec(memory_space=pltpu.VMEM)
PARAMS = pltpu.CompilerParams(vmem_limit_bytes=24 * 1024 * 1024)
WIDE = pltpu.CompilerParams(vmem_limit_bytes=62 * 1024 * 1024)


def halves(value):
    high = value.astype(BF16)
    return high, (value - high.astype(F32)).astype(BF16)


def product(left, right, dims):
    one = lambda a, b: lax.dot_general(a, b, (dims, ((), ())), preferred_element_type=F32)
    return one(left[0], right[0]) + (one(left[0], right[1]) + one(left[1], right[0]))


NN = ((1,), (0,))
TN = ((0,), (0,))
NT = ((1,), (1,))


def enter_kernel(count, *refs):
    data, second_ref, out_ref = refs[:count], refs[count], refs[count + 2]
    held, s_ref, made = refs[count + 3:2 * count + 3], refs[2 * count + 3], refs[2 * count + 4]
    data_sem, s_sem, out_sem = refs[2 * count + 5:]
    deep, xs, near, rows, width, channels = out_ref.shape
    half = s_ref.shape[0] // near

    def fetch(row):
        return [
            pltpu.make_async_copy(data[n].at[row], held[n].at[row], data_sem.at[n, row]) for n in range(count)
        ]

    fetches = [fetch(row) for row in range(rows)]
    factors = [
        pltpu.make_async_copy(second_ref.at[pl.ds(n * half, half)], s_ref.at[pl.ds(n * half, half)], s_sem.at[n])
        for n in range(near)
    ]
    for copy in fetches[0] + factors + [copy for row in fetches[1:] for copy in row]:
        copy.start()
    seconds = []
    sends = []
    for row in range(rows):
        for copy in fetches[row]:
            copy.wait()
        value = held[0][row]
        for ref in held[1:]:
            value = value * ref[row]
        value = halves(value)
        for n in range(near):
            if row == 0:
                factors[n].wait()
                seconds.append(halves(s_ref[n * half:(n + 1) * half]))
            got = product(seconds[n], value, NN)
            made[n, :, :, row] = got.reshape(xs, deep, width, channels)
            for x in range(xs):
                copy = pltpu.make_async_copy(made.at[n, x, :, row], out_ref.at[:, x, n, row], out_sem.at[row, n, x])
                copy.start()
                sends.append(copy)
    for copy in sends:
        copy.wait()


def enter(send, flops, factor, after, *data):
    count = len(data)
    deep, xs, near, rows, width, channels = send
    size = math.prod(send) + factor.size + sum(each.size for each in data)
    return pl.pallas_call(
        functools.partial(enter_kernel, count),
        out_shape=jax.ShapeDtypeStruct(send, F32),
        in_specs=[FAR] * (count + 1) + [UNREAD],
        out_specs=FAR,
        scratch_shapes=[pltpu.VMEM(each.shape, F32) for each in data]
        + [
            pltpu.VMEM(factor.shape, F32),
            pltpu.VMEM((near, xs, deep, rows, width, channels), F32),
            pltpu.SemaphoreType.DMA((count, rows)),
            pltpu.SemaphoreType.DMA((near,)),
            pltpu.SemaphoreType.DMA((rows, near, xs)),
        ],
        compiler_params=WIDE,
        cost_estimate=pl.CostEstimate(flops=flops, bytes_accessed=4 * size, transcendentals=0),
    )(*data, factor, after)


def lines(ref, row, nears):
    deep, xs, near, rows, width, channels = ref.shape
    return jnp.concatenate([ref[:, x, n, row].reshape(deep * width, channels) for n in nears for x in range(xs)], axis=0)


def forward_kernel(a_ref, k_ref, f_ref, v_ref):
    first = halves(f_ref[...])
    for k in range(a_ref.shape[1]):
        z = product(first, halves(a_ref[:, k]), NN)
        v_ref[:, k] = product(first, halves(k_ref[:, k] * z), TN)


def backward_kernel(shape, a_ref, d_ref, k_ref, f_ref, da_ref, gk_ref, gf_ref, lines_ref):
    first = halves(f_ref[...])
    total = jnp.zeros(lines_ref.shape, F32)
    for k in range(a_ref.shape[1]):
        dv = halves(d_ref[:, k])
        dw = product(first, dv, NN)
        section = halves(a_ref[:, k])
        z = product(first, section, NN)
        weight = k_ref[:, k]
        gk_ref[:, k] = dw * z
        dz = halves(weight * dw)
        da_ref[:, k] = product(first, dz, TN)
        total += product(dv, halves(weight * z), NT) + product(section, dz, NT)
    deep, xs, near, rows = shape
    for z in range(deep):
        for x in range(xs):
            for n in range(near):
                at = ((z * xs + x) * near + n) * rows
                to = ((n * xs + x) * deep + z) * rows
                lines_ref[to:to + rows] = total[at:at + rows]
    turned = lines_ref[...].T
    pieces, tall, lanes = gf_ref.shape
    low = turned.shape[0] // pieces
    gf_ref[...] = jnp.zeros(gf_ref.shape, F32)
    for piece in range(pieces):
        gf_ref[piece, :low] = turned[piece * low:(piece + 1) * low]


def leave_gates_kernel(v_ref, g_ref, c_ref, s_ref, gk_ref, gg_ref, gs_ref, same_ref):
    rows, block, channels = g_ref.shape
    second = halves(s_ref[...])
    total = jnp.zeros(gs_ref.shape, F32)
    for row in range(rows):
        v = halves(lines(v_ref, row, range(v_ref.shape[2])))
        gg_ref[row] = c_ref[row] * product(second, v, TN)
        total += product(v, halves(g_ref[row] * c_ref[row]), NT)
    gs_ref[...] = total


def half_outer(half, d_ref, x_ref, gs_ref, gf_ref, part, sem, packet):
    rows, block, channels = x_ref.shape
    pieces, tall, lanes = packet
    fetch = pltpu.make_async_copy(gs_ref.at[pl.ds(pl.multiple_of(half * (block // 2), block // 2), block // 2)], part, sem)
    fetch.start()
    total = jnp.zeros(part.shape, F32)
    for row in range(rows):
        total += product(halves(lines(d_ref, row, [half])), halves(x_ref[row]), NT)
    fetch.wait()
    total += part[...]
    high = block // (2 * pieces)
    strips = block // lanes
    return [
        (slice(strip * high, (strip + 1) * high), total[:, strip * lanes:(strip + 1) * lanes].reshape(pieces, high, lanes))
        for strip in range(strips)
    ] + [(slice(strips * high, tall), gf_ref[pl.ds(half * pieces, pieces)])]


def send_kernel(me_ref, d_ref, x_ref, gs_ref, gf_ref, after_ref, out_ref, part, sem):
    for rows, value in half_outer(1 - me_ref[0], d_ref, x_ref, gs_ref, gf_ref, part, sem, out_ref.shape):
        out_ref[:, rows] = value


def keep_kernel(me_ref, d_ref, x_ref, gs_ref, gf_ref, got_ref, out_ref, part, sem):
    for rows, value in half_outer(me_ref[0], d_ref, x_ref, gs_ref, gf_ref, part, sem, out_ref.shape):
        out_ref[:, rows] = value + got_ref[:, rows]


def sum_kernel(in_ref, after_ref, out_ref):
    total = in_ref[0]
    for part in range(1, in_ref.shape[0]):
        total += in_ref[part]
    out_ref[...] = jnp.broadcast_to(total[None], out_ref.shape)


def unpack_kernel(first_scale, second_scale, me_ref, mine_ref, other_ref, gf_ref, gs_ref):
    pieces, tall, lanes = mine_ref.shape
    block = gs_ref.shape[0]
    high = block // (2 * pieces)
    strips = block // lanes
    me = me_ref[0]
    for half, ref in ((me, mine_ref), (1 - me, other_ref)):
        rows = pl.ds(pl.multiple_of(half * (block // 2), block // 2), block // 2)
        for strip in range(strips):
            got = ref[:, strip * high:(strip + 1) * high].reshape(block // 2, lanes)
            gs_ref[rows, strip * lanes:(strip + 1) * lanes] = got * second_scale
    low = gf_ref.shape[0] // (2 * pieces)
    base = strips * high
    for piece in range(pieces):
        mine = mine_ref[piece, base:base + low] * first_scale
        other = other_ref[piece, base:base + low] * first_scale
        gf_ref[piece * low:(piece + 1) * low] = jnp.where(me == 0, mine, other)
        gf_ref[(piece + pieces) * low:(piece + pieces + 1) * low] = jnp.where(me == 0, other, mine)


def leave_signal_kernel(d_ref, s_ref, gx_ref, token_ref):
    token_ref[...] = jnp.zeros(token_ref.shape, F32)
    rows, block, channels = gx_ref.shape
    second = halves(s_ref[...])
    for row in range(rows):
        gx_ref[row] = product(second, halves(lines(d_ref, row, range(d_ref.shape[2]))), TN)


SCALAR = pl.BlockSpec(memory_space=pltpu.SMEM)
UNREAD = pl.BlockSpec(memory_space=pl.ANY)
FAR = pl.BlockSpec(memory_space=pltpu.HBM)


def call(kernel, outs, flops, *args, specs=None, out_specs=None, aliases=None, scratch=()):
    size = sum(math.prod(shape) for shape in outs) + sum(arg.size for arg in args)
    return pl.pallas_call(
        kernel,
        out_shape=[jax.ShapeDtypeStruct(shape, F32) for shape in outs],
        in_specs=specs or [VMEM] * len(args),
        out_specs=out_specs or [VMEM] * len(outs),
        input_output_aliases=aliases or {},
        scratch_shapes=list(scratch),
        compiler_params=PARAMS,
        cost_estimate=pl.CostEstimate(flops=flops, bytes_accessed=4 * size, transcendentals=0),
    )(*args)


def exchange(data, axes):
    return lax.all_to_all(data, axes, split_axis=0, concat_axis=0, tiled=True)


def swap(data, axis):
    return lax.ppermute(data, axis, [(0, 1), (1, 0)])


def pick(data, axis, index):
    return lax.dynamic_index_in_dim(data, index, axis, keepdims=False)


def halve_sum(data, axis, name):
    me = lax.axis_index(name)
    return pick(data, axis, me) + swap(pick(data, axis, 1 - me), name)


def solution(mesh):
    seq = ("near", "x", "z")
    order = ("z", "x", "near")
    dp = ("far", "core")
    shape = dict(mesh.shape)
    near = 2
    xs = 4
    fine = Mesh(
        mesh.devices.reshape(near, xs, shape["seq"] // (near * xs), shape["dp"] // 2, 2),
        seq + dp,
    )

    def body(signal, gate_values, cotangent, kernel, first_factor, second_factor):
        blocks = first_factor.shape[0]
        block = second_factor.shape[0]
        channels = signal.shape[2]
        peers = lax.axis_size(seq)
        rows = signal.shape[1] // block
        width = block // peers
        near, xs, deep = (lax.axis_size(name) for name in seq)
        send = (deep, xs, near, rows, width, channels)
        flat = (peers, rows, width, channels)
        side = (blocks, width, channels)
        place = (rows, block, channels)
        source = signal.reshape(place)
        gating = gate_values.reshape(place)
        upstream = cotangent.reshape(place)
        second_flops = 6 * rows * block * block * channels
        first_flops = 6 * blocks * blocks * width * channels
        turned = first_factor.reshape(blocks, near, xs, deep, rows).transpose(0, 3, 2, 1, 4).reshape(blocks, blocks)
        lanes = 128
        turn = jnp.zeros((8, lanes), F32)
        for _ in range(4):
            turn = lax.ppermute(turn, ("x", "core"), [(2 * x + 1, (2 * x + 3) % (2 * xs)) for x in range(xs)])
        section = enter(send, second_flops, second_factor, turn, source)
        across = ("near", "x", "far")
        pieces = lax.axis_size(across)
        low = -(-blocks // (16 * pieces)) * 8
        tall = block * block // (2 * lanes * pieces) + low
        section = exchange(section.reshape(flat), order).reshape(side)
        grad_back = enter(send, second_flops, second_factor, turn, gating, upstream)
        grad_back = exchange(grad_back.reshape(flat), order).reshape(side)
        (back,) = call(forward_kernel, [side], 2 * first_flops, section, kernel, turned)
        back = exchange(back.reshape(flat), order).reshape(send)
        grad_section, grad_kernel, grad_first = call(
            functools.partial(backward_kernel, (deep, xs, near, rows)),
            [side, side, (2 * pieces, low, lanes)],
            5 * first_flops,
            section,
            grad_back,
            kernel,
            turned,
            scratch=[pltpu.VMEM((blocks, blocks), F32)],
        )
        grad_section = exchange(grad_section.reshape(flat), order).reshape(send)
        grad_gate, second_part, grad_kernel = call(
            leave_gates_kernel,
            [place, (block, block), side],
            2 * second_flops,
            back,
            gating,
            upstream,
            second_factor,
            grad_kernel,
            specs=[VMEM] * 4 + [UNREAD],
            out_specs=[VMEM] * 2 + [UNREAD],
            aliases={4: 2},
        )
        sequences = lax.axis_size(dp)
        grad_kernel = grad_kernel.reshape(sequences // 2, 2, blocks // sequences, width, channels)
        kernel_pair = halve_sum(grad_kernel, 1, "core")
        grad_kernel = halve_sum(kernel_pair, 0, "far")
        me = lax.axis_index("core").reshape(1)
        packet = (pieces, tall, lanes)
        outer_args = (me, grad_section, source, second_part, grad_first)
        outer_specs = [SCALAR, VMEM, VMEM, FAR, VMEM]
        scratch = [pltpu.VMEM((block // 2, block), F32), pltpu.SemaphoreType.DMA]
        (half,) = call(
            send_kernel,
            [packet],
            second_flops // 2,
            *outer_args,
            kernel_pair[0, :1],
            specs=outer_specs + [UNREAD],
            scratch=scratch,
        )
        half = swap(half, "core")
        (half,) = call(
            keep_kernel, [packet], second_flops // 2, *outer_args, half, specs=outer_specs + [VMEM], scratch=scratch
        )
        grad_source, token = call(leave_signal_kernel, [place, (8, lanes)], second_flops, grad_section, second_factor)
        (part,) = call(sum_kernel, [(deep, tall, lanes)], 0, exchange(half, across), token, specs=[VMEM, UNREAD])
        part = exchange(part, "z")
        (part,) = call(sum_kernel, [packet], 0, part, grad_kernel[:1], specs=[VMEM, UNREAD])
        mine = exchange(part, across)
        other = swap(mine, "core")
        first_scale = 1.0 / math.sqrt(sequences * block * channels)
        second_scale = 1.0 / math.sqrt(sequences * blocks * channels)
        first_total, second_total = call(
            functools.partial(unpack_kernel, first_scale, second_scale),
            [(blocks, blocks), (block, block)],
            0,
            me,
            mine,
            other,
            specs=[SCALAR, VMEM, VMEM],
        )
        return (
            grad_source.reshape(signal.shape),
            grad_gate.reshape(signal.shape),
            grad_kernel,
            first_total,
            second_total,
        )

    wide = P(dp, seq, None)
    return jax.shard_map(
        body,
        mesh=fine,
        in_specs=(wide, wide, wide, P(None, seq, None), P(), P()),
        out_specs=(wide, wide, P(dp, seq, None), P(), P()),
        check_vma=False,
    )
```
